128 devices in a mesh: section: 4 (over x_hi, core), dp: 32 (over y, x_lo, z).
Axes of the slice: x: 4 (x_hi: 2, x_lo: 2; x = x_hi * 2 + x_lo), y: 4, z: 4, core: 2. Of those that a mesh axis runs over, the one named last changes fastest.
Arguments:
- inputs: bfloat16 [2, 2048, 8192], P(None, 'dp')
- cotangent: bfloat16 [2, 2048, 8192], P(None, 'dp'), may hold values from -6 to 6
- down_weight: bfloat16 [4, 8192, 128], P('section', 'dp'), may hold values from -0.0625 to 0.0625
- up_weight: bfloat16 [4, 8192, 128], P('section', 'dp'), may hold values from -0.5 to 0.5
- section_gains: bfloat16 [4, 8192], P('section'), may hold values from 0.5 to 1.5
- act_bases: bfloat16 [4, 2, 2, 2048, 8192], P('section', None, None, 'dp'), as said below
- grad_bases: bfloat16 [4, 2, 2, 2048, 8192], P('section', None, None, 'dp'), as said below
- slot_ids: int32 [32, 2], P('dp'), may hold values from 0 to 1, each once within a row
- act_exps: int32 [4, 2, 2048, 64], P('section', None, 'dp'), may hold values from 6 to 9
- grad_exps: int32 [4, 2, 2048, 64], P('section', None, 'dp'), may hold values from 6 to 9
Outputs:
- grad_down: float32 [4, 8192, 128], P('section', 'dp')
- grad_up: float32 [4, 8192, 128], P('section', 'dp')
The draws below stay inside these ranges and needn't reach their ends.
Inputs may be any that keep to these rules, and one draw needn't show every extreme that they name: Each row names every cache slot once: replica r's micro-batch m uses slot slot_ids[r, m]. act_bases[s, 1] equals act_bases[s + 1, 0] for every section s below 3. grad_bases[s, 0] equals grad_bases[s - 1, 1] for every section s from 1 on.
All inputs are finite; a program needn't handle non-finite values.
Results may differ from the reference program's by a relative error of at most 0.034.
Values may be sent and summed in bfloat16 or wider, within the bound.
A program may use at most 128 MiB of HBM per device.

```python
import math
import jax
import jax.numpy as jnp
from jax import lax

D = 8192
R = 128
MB = 2
TOKENS = 2048
SECTIONS = 4
REPLICAS = 32
BLOCKS = 64


def apply_scales(key, noise, low, high):
    row_key, column_key = jax.random.split(key)
    row_shape = noise.shape[:-1] + (1,)
    column_shape = (1,) * (noise.ndim - 1) + (noise.shape[-1],)
    rows = jnp.exp(jax.random.uniform(row_key, row_shape, jnp.float32, jnp.log(low), jnp.log(high)))
    columns = jnp.exp(jax.random.uniform(column_key, column_shape, jnp.float32, jnp.log(low), jnp.log(high)))
    return noise * rows * columns


def draw_inputs(key, part):
    key = jax.random.fold_in(key, 11)
    noise_key, scale_key = jax.random.split(key)
    full_shape = (MB, TOKENS, D)
    noise = jax.random.normal(noise_key, full_shape, jnp.float32)
    return apply_scales(scale_key, noise, 0.4, 2.5).astype(jnp.bfloat16)


def draw_act_bases(key, part):
    key = jax.random.fold_in(key, 12)
    noise_key, scale_key = jax.random.split(key)
    full_shape = (SECTIONS + 1, MB, TOKENS, D)
    noise = jax.random.normal(noise_key, full_shape, jnp.float32)
    table = apply_scales(scale_key, noise, 0.4, 2.5)
    return jnp.stack([table[:-1], table[1:]], axis=1).astype(jnp.bfloat16)


def draw_grad_bases(key, part):
    key = jax.random.fold_in(key, 13)
    noise_key, scale_key = jax.random.split(key)
    full_shape = (SECTIONS + 1, MB, TOKENS, D)
    noise = jax.random.normal(noise_key, full_shape, jnp.float32)
    table = apply_scales(scale_key, noise, 0.4, 2.5)
    return jnp.stack([table[:-1], table[1:]], axis=1).astype(jnp.bfloat16)


def touch_ends(drawn, stream_key, low, high):
    index_at = [jax.random.randint(jax.random.fold_in(stream_key, axis), (), 0, length) for axis, length in enumerate(drawn.shape)]
    widest = drawn.shape.index(max(drawn.shape))
    next_to = index_at[:widest] + [(index_at[widest] + 1) % drawn.shape[widest]] + index_at[widest + 1:]
    return drawn.at[tuple(index_at)].set(low).at[tuple(next_to)].set(high)


def strengthened(result, key, source, target, blocks, factor):
    def block_of(axis_at):
        return (jnp.arange(result.shape[axis_at]) // (result.shape[axis_at] // blocks)).reshape((-1,) + (1,) * (result.ndim - 1 - axis_at))

    first = jax.random.permutation(key, blocks)[block_of(target)]
    second = (block_of(target) + blocks // 2) % blocks
    return jnp.where((block_of(source) == first) | (block_of(source) == second), factor * result, result)


def shard_levels(stream_key, extent, cuts, least, high):
    level, own = 1.0, jax.random.fold_in(stream_key, 6)
    for position, shards_of in cuts:
        steps = jnp.exp(jax.random.uniform(jax.random.fold_in(own, position), (shards_of,), jnp.float32, least / len(cuts), high / len(cuts)))
        level = level * jnp.repeat(steps, extent[position] // shards_of).reshape([-1 if axis == position else 1 for axis in range(len(extent))])
    return level


def scatter_about(own_key, extent, scale, limit, cuts=(), kind=jnp.bfloat16):
    level = shard_levels(own_key, extent, cuts, -0.22, 0.18) if cuts else 1.0
    values = jax.random.normal(own_key, extent, jnp.float32) * scale * level
    return jnp.minimum(jnp.maximum(values, -limit), limit).astype(kind)


def noise_with(rng, extent, spread, bound, cuts, heavy, kind=jnp.bfloat16):
    drawn = spread * jax.random.normal(rng, extent, jnp.float32)
    if cuts:
        drawn = drawn * shard_levels(rng, extent, cuts, -0.22, 0.18)
    return jnp.clip(strengthened(drawn, jax.random.fold_in(rng, 3), *heavy), -bound, bound).astype(kind)


def setup_inputs(seed: int = 0) -> dict:
    key_list = jax.random.split(jax.random.key(seed), 11)
    inputs = draw_inputs(jax.random.fold_in(key_list[10], 71), 0)
    cotangent = noise_with(key_list[1], (MB, TOKENS, D), 1.0, 6.0, ((1, 32),), (1, 2, 32, 2.75))
    down_weight = scatter_about(key_list[2], (SECTIONS, D, R), D ** -0.5, 0.0625, ((0, 4), (1, 32)))
    up_weight = scatter_about(key_list[3], (SECTIONS, D, R), R ** -0.5, 0.5, ((0, 4), (1, 32)))
    section_gains = jnp.clip(1.0 + 0.1 * jax.random.normal(key_list[4], (SECTIONS, D), jnp.float32), 0.5, 1.5).astype(jnp.bfloat16)
    act_bases = draw_act_bases(jax.random.fold_in(key_list[10], 71), 0)
    grad_bases = draw_grad_bases(jax.random.fold_in(key_list[10], 71), 0)
    slot_ids = jax.vmap(lambda own: jax.random.permutation(own, MB))(jax.random.split(key_list[7], REPLICAS)).reshape((REPLICAS, MB)).astype(jnp.int32)
    act_exps = touch_ends(jax.random.randint(key_list[8], (SECTIONS, MB, TOKENS, BLOCKS), 6, 10), jax.random.fold_in(key_list[8], 1), 6, 9).astype(jnp.int32)
    grad_exps = touch_ends(jax.random.randint(key_list[9], (SECTIONS, MB, TOKENS, BLOCKS), 6, 10), jax.random.fold_in(key_list[9], 1), 6, 9).astype(jnp.int32)
    return dict(inputs=inputs, cotangent=cotangent, down_weight=down_weight, up_weight=up_weight, section_gains=section_gains, act_bases=act_bases, grad_bases=grad_bases, slot_ids=slot_ids, act_exps=act_exps, grad_exps=grad_exps)


code_limit = 448.0
norm_eps = 1e-05

def power_table(exponents, direction_sign):
    factors = jnp.zeros(exponents.shape, jnp.float32)
    for exponent in range(6, 10):
        factors = jnp.where(exponents == exponent, jnp.float32(2.0 ** (direction_sign * exponent)), factors)
    return factors

def encode(delta, exponents):
    full_shape = delta.shape
    grouped = delta.reshape(full_shape[:-1] + (exponents.shape[-1], full_shape[-1] // exponents.shape[-1]))
    scaled = grouped * power_table(exponents, 1)[..., None]
    return jnp.clip(scaled, -code_limit, code_limit).astype(jnp.bfloat16).reshape(full_shape)

def decode(base, codes, exponents):
    full_shape = codes.shape
    grouped = codes.astype(jnp.float32).reshape(full_shape[:-1] + (exponents.shape[-1], full_shape[-1] // exponents.shape[-1]))
    restored = (grouped * power_table(exponents, -1)[..., None]).reshape(full_shape)
    return (base.astype(jnp.float32) + restored).astype(jnp.bfloat16)

def section_forward(section_input, down_full, up_full, gain):
    full_input = section_input.astype(jnp.float32)
    inverse = lax.rsqrt(lax.optimization_barrier(jnp.mean(full_input * full_input, axis=-1, keepdims=True)) + norm_eps)
    normed = (full_input * inverse * gain.astype(jnp.float32)).astype(jnp.bfloat16)
    inner = jnp.dot(normed, down_full, preferred_element_type=jnp.float32)
    hidden = jax.nn.silu(inner).astype(jnp.bfloat16)
    output = full_input + jnp.dot(hidden, up_full.T, preferred_element_type=jnp.float32)
    return (output, (full_input, inverse, normed, inner, hidden))

def section_backward(upstream, pieces, down_full, up_full, gain):
    full_input, inverse, normed, inner, hidden = pieces
    back_hidden = jnp.dot(upstream, up_full, preferred_element_type=jnp.float32)
    sigma = jax.nn.sigmoid(inner)
    back_inner = (back_hidden * sigma * (1.0 + inner * (1.0 - sigma))).astype(jnp.bfloat16)
    back_normed = jnp.dot(back_inner, down_full.T, preferred_element_type=jnp.float32) * gain.astype(jnp.float32)
    back_input = upstream.astype(jnp.float32) + inverse * back_normed - full_input * inverse ** 3 * lax.optimization_barrier(jnp.mean(back_normed * full_input, axis=-1, keepdims=True))
    return (back_input, back_inner)

def pick_slot(table, slot_ids, micro_index):
    slot_count, token_count, model_width = table.shape
    grouped = table.reshape(slot_count, REPLICAS, token_count // REPLICAS, model_width)
    chosen = grouped[slot_ids[:, micro_index], jnp.arange(REPLICAS, dtype=jnp.int32)]
    return chosen.reshape(token_count, model_width)

def reference(inputs, cotangent, down_weight, up_weight, section_gains, act_bases, grad_bases, slot_ids, act_exps, grad_exps):
    saved = []
    for micro_index in range(MB):
        section_input = inputs[micro_index]
        section_row = []
        for section_number in range(SECTIONS):
            section_row.append(section_input)
            if section_number + 1 < SECTIONS:
                output, pieces = section_forward(section_input, down_weight[section_number], up_weight[section_number], section_gains[section_number])
                base_out = pick_slot(act_bases[section_number, 1], slot_ids, micro_index).astype(jnp.float32)
                codes = encode(output - base_out, act_exps[section_number, micro_index])
                codes = lax.optimization_barrier(codes)
                base_in = pick_slot(act_bases[section_number + 1, 0], slot_ids, micro_index)
                section_input = decode(base_in, codes, act_exps[section_number, micro_index])
        saved.append(section_row)
    down_totals = [jnp.zeros((D, R), jnp.float32) for section_number in range(SECTIONS)]
    up_totals = [jnp.zeros((D, R), jnp.float32) for section_number in range(SECTIONS)]
    for micro_index in range(MB):
        upstream = cotangent[micro_index]
        for section_number in reversed(range(SECTIONS)):
            down_full = down_weight[section_number]
            up_full = up_weight[section_number]
            gain = section_gains[section_number]
            pieces = section_forward(saved[micro_index][section_number], down_full, up_full, gain)[1]
            back_input, back_inner = section_backward(upstream, pieces, down_full, up_full, gain)
            down_totals[section_number] = down_totals[section_number] + jnp.dot(pieces[2].T, back_inner, preferred_element_type=jnp.float32)
            up_totals[section_number] = up_totals[section_number] + jnp.dot(upstream.T, pieces[4], preferred_element_type=jnp.float32)
            if section_number > 0:
                base_out = pick_slot(grad_bases[section_number, 0], slot_ids, micro_index).astype(jnp.float32)
                codes = encode(back_input - base_out, grad_exps[section_number, micro_index])
                codes = lax.optimization_barrier(codes)
                base_in = pick_slot(grad_bases[section_number - 1, 1], slot_ids, micro_index)
                upstream = decode(base_in, codes, grad_exps[section_number, micro_index])
    grad_scale = 1.0 / math.sqrt(MB * TOKENS)
    return (jnp.stack(down_totals) * grad_scale, jnp.stack(up_totals) * grad_scale)
```

```python
import functools
import math

import jax
import jax.numpy as jnp
from jax import lax
from jax.experimental import pallas as pl
from jax.experimental.pallas import tpu as pltpu
from jax.sharding import PartitionSpec as P

MESH = pl.DeviceIdType.MESH
F32 = jnp.float32
BF16 = jnp.bfloat16

SECTIONS = 4
WIDTH = 8192
RANK = 128
TOK = 64
ROWS = 2 * TOK
CH = 256
CHUNKS = 8
NORM_EPS = 1e-05
OFF = (1, 3, 2)
DOWN, UP = 0, 1


def dot(a, b):
    return jnp.dot(a, b, preferred_element_type=F32)


def dot_t(a, b):
    return lax.dot_general(a, b, (((1,), (1,)), ((), ())), preferred_element_type=F32)


def kernel(
    x_hbm,
    ct_hbm,
    dw_hbm,
    uw_hbm,
    ab_hbm,
    gb_hbm,
    gain_ref,
    lim_ref,
    slot_ref,
    od_ref,
    ou_ref,
    W,
    acts,
    ups,
    TB,
    GB,
    gains,
    lims,
    sel,
    xs,
    xr,
    inner_all,
    inv_all,
    hid_all,
    bis_all,
    G,
    R1d,
    R1u,
    S1d,
    S1u,
    R2,
    S2,
    R3,
    loc_sem,
    base_s,
    base_r,
    small_s,
    small_r,
    p0_s,
    p0_r,
    p1_s,
    p1_r,
    p2_s,
    p2_r,
    r1_s,
    r1_r,
    r2_s,
    r2_r,
    r3_s,
    r3_r,
    x_s,
    x_r,
):
    S, J = lax.axis_index("section"), lax.axis_index("dp")
    xh, c = S // 2, S % 2
    y, xl, z = J // 8, (J // 4) % 2, J % 4
    i_own = z // 2
    src = (z % 2) == c
    not_src = (z % 2) != c

    def dp(yy, xx, zz):
        return yy * 8 + xx * 4 + zz

    def at_y(o):
        return (S, dp((y + o) % 4, xl, z))

    def at_z(o):
        return (S, dp(y, xl, (z + o) % 4))

    def group(e):
        return ((S + e) % 4, J)

    p0_sec = xl * 2 + z % 2

    def p0_dev(xx):
        return (p0_sec, dp(y, xx, z))

    def p0_self(xx):
        return (p0_sec == S) & (xl == xx)

    def owner(s):
        return (s, dp(y, xh, z))

    def owner_self(s):
        return (S == s) & (xl == xh)

    def feat(kk, h, cc):
        return (kk // 2) * 2048 + h * 1024 + ((kk % 2) * 2 + cc) * 256

    def remote(a, b, ss, rs, dev):
        return pltpu.make_async_remote_copy(
            src_ref=a, dst_ref=b, send_sem=ss, recv_sem=rs, device_id=dev, device_id_type=MESH
        )

    def arrived(ref, rs):
        remote(ref, ref, rs, rs, (S, J)).wait_recv()

    def sent(ref, ss):
        remote(ref, ref, ss, ss, (S, J)).wait_send()

    def local_done(ref, sem):
        pltpu.make_async_copy(ref, ref, sem).wait()

    barrier = pltpu.get_barrier_semaphore()

    def greet(dev):
        pl.semaphore_signal(barrier, inc=1, device_id=dev, device_id_type=MESH)

    for e in (1, 2, 3):
        greet(group(e))
        greet(at_y(e))
        greet(at_z(e))
    for xx in (0, 1):
        @pl.when(jnp.logical_not(p0_self(xx)))
        def _():
            greet(p0_dev(xx))
    for s in range(SECTIONS):
        @pl.when(src & jnp.logical_not(owner_self(s)))
        def _():
            greet(owner(s))

    def load(ref_of, dst, sem, h, cc):
        def step(kk, _):
            pltpu.make_async_copy(
                ref_of.at[:, pl.ds(pl.multiple_of(feat(kk, h, cc), 256), CH)], dst.at[kk], sem
            ).start()
            return 0

        lax.fori_loop(0, CHUNKS, step, 0)

    def push(ref_of, dst, ss, rs, h, cc, dev):
        def step(kk, _):
            remote(
                ref_of.at[:, pl.ds(pl.multiple_of(feat(kk, h, cc), 256), CH)],
                dst.at[kk],
                ss,
                rs,
                dev,
            ).start()
            return 0

        lax.fori_loop(0, CHUNKS, step, 0)

    near = 2 * xh
    far = 2 - near
    holds_mid = c != xh
    lacks_mid = c == xh
    load(x_hbm, acts.at[0], loc_sem.at[0], xh, c)

    is_self0 = jnp.where(p0_self(0) | p0_self(1), 1, 0)
    own_any = jnp.where(xl == xh, 1, 0)
    n_greet = 9 + 2 - is_self0 + jnp.where(src, 4 - own_any, 0)
    pl.semaphore_wait(barrier, n_greet)

    for xx in (0, 1):
        for mat, ref in ((DOWN, dw_hbm), (UP, uw_hbm)):
            there = W.at[S, mat, y, i_own]

            @pl.when(jnp.logical_not(p0_self(xx)))
            def _():
                remote(ref, there, p0_s.at[xx, mat], p0_r.at[S, mat], p0_dev(xx)).start()

            @pl.when(p0_self(xx))
            def _():
                pltpu.make_async_copy(ref, there, p0_r.at[S, mat]).start()

    for e in (1, 2, 3):
        remote(gain_ref, gains.at[S], small_s.at[e - 1, 0], small_r.at[e - 1, 0], group(e)).start()
        remote(lim_ref, lims.at[S], small_s.at[e - 1, 1], small_r.at[e - 1, 1], group(e)).start()

    cross = (S + 2) % 4
    sib = xh * 2 + (1 - c)
    push(ab_hbm.at[1 - c], TB.at[near], base_s.at[0], base_r.at[0], 1 - xh, c, (cross, J))
    load(ab_hbm.at[1 - c], TB.at[near], loc_sem.at[2], xh, c)

    @pl.when(holds_mid)
    def _():
        push(ab_hbm.at[c], TB.at[1], base_s.at[1], base_r.at[1], xh, 1 - c, (sib, J))
        load(ab_hbm.at[c], TB.at[1], loc_sem.at[3], xh, c)

    load(ct_hbm, ups.at[3], loc_sem.at[1], xh, c)
    push(gb_hbm.at[1 - c], GB.at[near], base_s.at[2], base_r.at[2], 1 - xh, c, (cross, J))
    load(gb_hbm.at[1 - c], GB.at[near], loc_sem.at[4], xh, c)

    @pl.when(holds_mid)
    def _():
        push(gb_hbm.at[c], GB.at[1], base_s.at[3], base_r.at[3], xh, 1 - c, (sib, J))
        load(gb_hbm.at[c], GB.at[1], loc_sem.at[5], xh, c)

    gains[S] = gain_ref[...]
    lims[S] = lim_ref[...]

    def build_sel(kk, _):
        b0 = (kk // 2) * 16 + xh * 8 + (kk % 2) * 4 + c * 2
        row = lax.broadcasted_iota(jnp.int32, (128, CH), 0)
        blk = lax.broadcasted_iota(jnp.int32, (128, CH), 1) // 128 + b0
        sel[0, kk] = jnp.where(row == blk, 1.0, 0.0).astype(BF16)
        sel[1, kk] = jnp.where(row == blk + 64, 1.0, 0.0).astype(BF16)
        return 0

    lax.fori_loop(0, CHUNKS, build_sel, 0)

    def p1_send(s):
        @pl.when(src)
        def _():
            for mat in (DOWN, UP):
                arrived(W.at[s, mat, y, i_own], p0_r.at[s, mat])
            for d, o in enumerate(OFF):
                w = W.at[s, DOWN, y, i_own]
                remote(w, w, p1_s.at[s, DOWN, d], p1_r.at[s, DOWN, d], at_y(o)).start()
                w = W.at[s, UP, y, i_own]
                remote(w, w, p1_s.at[s, UP, d], p1_r.at[s, UP, d], at_z(o)).start()

    def from_z(o):
        return ((z + 4 - o) % 4) // 2

    def z_arrive(view, sems):
        @pl.when(src)
        def _():
            arrived(view(from_z(OFF[2])), sems.at[2])

        @pl.when(not_src)
        def _():
            arrived(view(from_z(OFF[0])), sems.at[0])
            arrived(view(from_z(OFF[1])), sems.at[1])

    def p2_send(s):
        @pl.when(src)
        def _():
            for d, o in enumerate(OFF):
                arrived(W.at[s, DOWN, (y + 4 - o) % 4, i_own], p1_r.at[s, DOWN, d])
            for d, o in enumerate(OFF):
                w = W.at[s, DOWN, :, i_own]
                remote(w, w, p2_s.at[s, DOWN, d], p2_r.at[s, DOWN, d], at_z(o)).start()

        z_arrive(lambda i: W.at[s, UP, y, i], p1_r.at[s, UP])
        for d, o in enumerate(OFF):
            w = W.at[s, UP, y]
            remote(w, w, p2_s.at[s, UP, d], p2_r.at[s, UP, d], at_y(o)).start()

    def down_ready(s):
        z_arrive(lambda i: W.at[s, DOWN, :, i], p2_r.at[s, DOWN])

    def up_ready(s):
        for d, o in enumerate(OFF):
            arrived(W.at[s, UP, (y + 4 - o) % 4], p2_r.at[s, UP, d])

    def rows(m):
        return pl.ds(m * TOK, TOK)

    def gain_row(s, kk):
        return gains[s, pl.ds((kk // 2) * 8 + xh * 4 + (kk % 2) * 2 + c, 1), :]

    def fold(v):
        return v[:, :128] + v[:, 128:]

    def chunk_loop(step, init):
        return lax.fori_loop(0, CHUNKS, step, init, unroll=True)

    def x_send(ex, m):
        for e in (1, 2, 3):
            remote(
                xs.at[ex, m], xr.at[ex, m, e - 1], x_s.at[ex, m, e - 1], x_r.at[ex, m, e - 1], group(e)
            ).start()

    def x_total(ex, m, part):
        total = xs[ex, m, part].astype(F32)
        for e in range(3):
            total = total + xr[ex, m, e, part].astype(F32)
        return total

    def x_wait(ex, m):
        for e in range(3):
            arrived(xr.at[ex, m, e], x_r.at[ex, m, e])

    zero = jnp.zeros((TOK, 128), F32)

    def enter(s, kk, value, inner, sq):
        full = value.astype(F32)
        sq = sq + fold(full * full)
        scaled = (full * gain_row(s, kk)).astype(BF16)
        return inner + dot(scaled, W[s, DOWN, kk // 2, kk % 2]), sq

    def hand_over(ex, m, a, b):
        xs[ex, m, 0] = a.astype(BF16)
        xs[ex, m, 1] = b.astype(BF16)
        x_send(ex, m)

    def first(m):
        def step(kk, carry):
            return enter(0, kk, acts[0, kk, rows(m), :], *carry)

        inner, sq = chunk_loop(step, (zero, zero))
        hand_over(0, m, inner, sq)

    def activate(s, m):
        x_wait(s, m)
        mean = jnp.sum(x_total(s, m, 1), axis=-1, keepdims=True) * (1.0 / WIDTH)
        inv = jnp.broadcast_to(lax.rsqrt(mean + NORM_EPS), (TOK, 128))
        inner = x_total(s, m, 0) * inv
        hid = (inner * jax.nn.sigmoid(inner)).astype(BF16)
        inner_all[s, rows(m), :] = inner
        inv_all[s, rows(m), :] = inv
        hid_all[s, rows(m), :] = hid
        return hid

    def recode(value, table, b, m, kk, limit):
        use_first = jnp.broadcast_to(slot_ref[0:1, :], (TOK, CH)) == m
        base = jnp.where(
            use_first, table[b, kk, 0:TOK, :].astype(F32), table[b, kk, TOK:ROWS, :].astype(F32)
        )
        delta = jnp.minimum(jnp.maximum(value - base, -limit), limit).astype(BF16)
        return (base + delta.astype(F32)).astype(BF16)

    def forward(s, m):
        hid = activate(s, m)
        table = lims[s, rows(m), :]

        def step(kk, carry):
            out = acts[s, kk, rows(m), :].astype(F32) + dot_t(hid, W[s, UP, kk // 2, kk % 2])
            value = recode(out, TB, s, m, kk, dot(table, sel[0, kk]))
            acts[s + 1, kk, rows(m), :] = value
            return enter(s + 1, kk, value, *carry)

        inner, sq = chunk_loop(step, (zero, zero))
        hand_over(s + 1, m, inner, sq)

    def back_first(m):
        def step(kk, carry):
            return carry + dot(ups[3, kk, rows(m), :], W[3, UP, kk // 2, kk % 2])

        xs[4 + 3, m, 0] = chunk_loop(step, zero).astype(BF16)
        xb_send(3, m)

    def xb_send(s, m):
        for e in (1, 2, 3):
            remote(
                xs.at[4 + s, m, 0],
                xr.at[4 + s, m, e - 1, 0],
                x_s.at[4 + s, m, e - 1],
                x_r.at[4 + s, m, e - 1],
                group(e),
            ).start()

    def back_inner(s, m):
        for e in range(3):
            arrived(xr.at[4 + s, m, e, 0], x_r.at[4 + s, m, e])
        inner, inv = inner_all[s, rows(m), :], inv_all[s, rows(m), :]
        sig = jax.nn.sigmoid(inner)
        bi = x_total(4 + s, m, 0) * sig * (1.0 + inner * (1.0 - sig)) * inv
        bis = bi.astype(BF16)
        bis_all[s, rows(m), :] = bis
        coef = jnp.sum(bis.astype(F32) * inner * inv, axis=-1, keepdims=True) * (1.0 / WIDTH)
        return bis, jnp.broadcast_to(coef, (TOK, CH))

    def backward(s, m):
        bis, coef = back_inner(s, m)
        table = lims[s, rows(m), :]

        def step(kk, carry):
            back = dot_t(bis, W[s, DOWN, kk // 2, kk % 2]) * gain_row(s, kk)
            value = (
                ups[s, kk, rows(m), :].astype(F32)
                + back
                - acts[s, kk, rows(m), :].astype(F32) * coef
            )
            value = recode(value, GB, s - 1, m, kk, dot(table, sel[1, kk]))
            ups[s - 1, kk, rows(m), :] = value
            return carry + dot(value, W[s - 1, UP, kk // 2, kk % 2])

        xs[4 + s - 1, m, 0] = chunk_loop(step, zero).astype(BF16)
        xb_send(s - 1, m)

    def grad_up(s):
        left = jnp.transpose(hid_all[s].astype(F32)).astype(BF16)

        def step(kk, _):
            G[s, UP, kk // 2, kk % 2] = dot(left, ups[s, kk]).astype(BF16)
            return 0

        chunk_loop(step, 0)
        for d, o in enumerate(OFF):
            remote(
                G.at[s, UP, (y + o) % 4], R1u.at[s, d], r1_s.at[s, UP, d], r1_r.at[s, UP, d], at_y(o)
            ).start()

    def to_z(o):
        return ((z + o) % 4) // 2

    def z_give(view, there, ss, rs):
        def give(d):
            o = OFF[d]
            remote(view(to_z(o)), there.at[d], ss.at[d], rs.at[d], at_z(o)).start()

        @pl.when(src)
        def _():
            give(2)

        @pl.when(not_src)
        def _():
            give(0)
            give(1)

    def z_given(view, ss):
        @pl.when(src)
        def _():
            sent(view, ss.at[2])

        @pl.when(not_src)
        def _():
            sent(view, ss.at[0])
            sent(view, ss.at[1])

    def grad_down(s):
        left = jnp.transpose(bis_all[s].astype(F32)).astype(BF16)

        def step(kk, _):
            G[s, DOWN, kk // 2, kk % 2] = (dot(left, acts[s, kk]) * gain_row(s, kk)).astype(BF16)
            return 0

        chunk_loop(step, 0)
        z_give(lambda i: G.at[s, DOWN, :, i], R1d.at[s], r1_s.at[s, DOWN], r1_r.at[s, DOWN])

    def add4(a, b):
        return (
            a.astype(F32) + b[0].astype(F32) + (b[1].astype(F32) + b[2].astype(F32))
        ).astype(BF16)

    def r2_up(s):
        for d in range(3):
            arrived(R1u.at[s, d], r1_r.at[s, UP, d])
        for i in range(2):
            S1u[s, i] = add4(G[s, UP, y, i], [R1u[s, d, i] for d in range(3)])
        z_give(lambda i: S1u.at[s, i], R2.at[s, UP], r2_s.at[s, UP], r2_r.at[s, UP])

    def r2_down(s):
        @pl.when(src)
        def _():
            for d in range(3):
                arrived(R1d.at[s, d], r1_r.at[s, DOWN, d])
            for yy in range(4):
                S1d[s, yy] = add4(G[s, DOWN, yy, i_own], [R1d[s, d, yy] for d in range(3)])
            for d, o in enumerate(OFF):
                remote(
                    S1d.at[s, (y + o) % 4],
                    R2.at[s, DOWN, d],
                    r2_s.at[s, DOWN, d],
                    r2_r.at[s, DOWN, d],
                    at_y(o),
                ).start()

    def r3(s, mat):
        @pl.when(src)
        def _():
            for d in range(3):
                arrived(R2.at[s, mat, d], r2_r.at[s, mat, d])
            own = S1u[s, i_own] if mat == UP else S1d[s, y]
            S2[s, mat] = add4(own, [R2[s, mat, d] for d in range(3)])

            @pl.when(jnp.logical_not(owner_self(s)))
            def _():
                remote(
                    S2.at[s, mat], R3.at[xl, mat], r3_s.at[s, mat], r3_r.at[xl, mat], owner(s)
                ).start()

            @pl.when(owner_self(s))
            def _():
                pltpu.make_async_copy(S2.at[s, mat], R3.at[xl, mat], r3_r.at[xl, mat]).start()

    for s in range(SECTIONS):
        p1_send(s)
    for s in range(SECTIONS):
        p2_send(s)
    for e in (1, 2, 3):
        arrived(gains.at[(S + 4 - e) % 4], small_r.at[e - 1, 0])
        arrived(lims.at[(S + 4 - e) % 4], small_r.at[e - 1, 1])
    local_done(acts.at[0], loc_sem.at[0])
    down_ready(0)
    first(0)
    first(1)

    def base_ready(table, b, near_sem, mid_sem, far_sem, mid_far_sem):
        if b == 1:
            @pl.when(holds_mid)
            def _():
                local_done(table.at[1], mid_sem)

            @pl.when(lacks_mid)
            def _():
                arrived(table.at[1], mid_far_sem)
        else:
            @pl.when(near == b)
            def _():
                local_done(table.at[b], near_sem)

            @pl.when(near != b)
            def _():
                arrived(table.at[b], far_sem)

    for s in range(SECTIONS - 1):
        up_ready(s)
        base_ready(TB, s, loc_sem.at[2], loc_sem.at[3], base_r.at[0], base_r.at[1])
        down_ready(s + 1)
        forward(s, 0)
        forward(s, 1)
    up_ready(3)
    local_done(ups.at[3], loc_sem.at[1])
    back_first(0)
    back_first(1)
    activate(3, 0)
    activate(3, 1)
    grad_up(3)
    for s in (3, 2, 1):
        base_ready(GB, s - 1, loc_sem.at[4], loc_sem.at[5], base_r.at[2], base_r.at[3])
        backward(s, 0)
        backward(s, 1)
        grad_down(s)
        grad_up(s - 1)
        if s < 3:
            r2_up(s + 1)
            r2_down(s + 1)
        if s < 2:
            r3(s + 2, UP)
            r3(s + 2, DOWN)
    back_inner(0, 0)
    back_inner(0, 1)
    grad_down(0)
    r2_up(0)
    r2_up(1)
    r2_down(1)
    r3(2, UP)
    r3(2, DOWN)
    r2_down(0)
    r3(1, UP)
    r3(1, DOWN)
    r3(0, UP)
    r3(0, DOWN)

    scale = 1.0 / math.sqrt(2 * 2048)
    for mat, out in ((UP, ou_ref), (DOWN, od_ref)):
        for xx in (0, 1):
            arrived(R3.at[xx, mat], r3_r.at[xx, mat])
        total = (R3[0, mat].astype(F32) + R3[1, mat].astype(F32)) * scale
        out[...] = jnp.transpose(total)

    for xx in (0, 1):
        @pl.when(jnp.logical_not(p0_self(xx)))
        def _():
            for mat, ref in ((DOWN, dw_hbm), (UP, uw_hbm)):
                sent(ref, p0_s.at[xx, mat])
    for e in range(3):
        sent(gain_ref, small_s.at[e, 0])
        sent(lim_ref, small_s.at[e, 1])
    sent(TB.at[0], base_s.at[0])
    sent(GB.at[0], base_s.at[2])

    @pl.when(holds_mid)
    def _():
        sent(TB.at[1], base_s.at[1])
        sent(GB.at[1], base_s.at[3])

    def drain(s, _):
        @pl.when(src)
        def _():
            for d in range(3):
                sent(W.at[s, DOWN, y, i_own], p1_s.at[s, DOWN, d])
                sent(W.at[s, UP, y, i_own], p1_s.at[s, UP, d])
                sent(W.at[s, DOWN, :, i_own], p2_s.at[s, DOWN, d])
                sent(S1d.at[s, 0], r2_s.at[s, DOWN, d])

            @pl.when(jnp.logical_not(owner_self(s)))
            def _():
                for mat in (DOWN, UP):
                    sent(S2.at[s, mat], r3_s.at[s, mat])

        for d in range(3):
            sent(W.at[s, UP, y], p2_s.at[s, UP, d])
            sent(G.at[s, UP, 0], r1_s.at[s, UP, d])
        z_given(G.at[s, DOWN, :, 0], r1_s.at[s, DOWN])
        z_given(S1u.at[s, 0], r2_s.at[s, UP])
        for m in (0, 1):
            for e in range(3):
                sent(xs.at[s, m], x_s.at[s, m, e])
                sent(xs.at[4 + s, m, 0], x_s.at[4 + s, m, e])
        return 0

    lax.fori_loop(0, SECTIONS, drain, 0)


def body(
    inputs,
    cotangent,
    down_weight,
    up_weight,
    section_gains,
    act_bases,
    grad_bases,
    slot_ids,
    act_exps,
    grad_exps,
):
    def limits(exps):
        out = jnp.full(exps.shape, 448.0 * 2.0**-6, F32)
        for e in (7, 8, 9):
            out = jnp.where(exps == e, 448.0 * 2.0**-e, out)
        return out.reshape(ROWS, 64).astype(BF16)

    lim = jnp.concatenate([limits(act_exps), limits(grad_exps)], axis=1)
    gain = section_gains.astype(F32).reshape(32, CH)
    slot = jnp.broadcast_to(slot_ids[0, 0], (8, CH))
    any_spec = pl.BlockSpec(memory_space=pl.ANY)
    vmem = pl.BlockSpec(memory_space=pltpu.VMEM)
    dma = pltpu.SemaphoreType.DMA
    grad_down, grad_up = pl.pallas_call(
        kernel,
        out_shape=(jax.ShapeDtypeStruct((CH, RANK), F32),) * 2,
        in_specs=[any_spec] * 6 + [vmem] * 3,
        out_specs=(vmem, vmem),
        scratch_shapes=[
            pltpu.VMEM((4, 2, 4, 2, CH, RANK), BF16),
            pltpu.VMEM((4, CHUNKS, ROWS, CH), BF16),
            pltpu.VMEM((4, CHUNKS, ROWS, CH), BF16),
            pltpu.VMEM((3, CHUNKS, ROWS, CH), BF16),
            pltpu.VMEM((3, CHUNKS, ROWS, CH), BF16),
            pltpu.VMEM((4, 32, CH), F32),
            pltpu.VMEM((4, ROWS, 128), BF16),
            pltpu.VMEM((2, CHUNKS, 128, CH), BF16),
            pltpu.VMEM((8, 2, 2, TOK, 128), BF16),
            pltpu.VMEM((8, 2, 3, 2, TOK, 128), BF16),
            pltpu.VMEM((4, ROWS, RANK), F32),
            pltpu.VMEM((4, ROWS, RANK), F32),
            pltpu.VMEM((4, ROWS, RANK), BF16),
            pltpu.VMEM((4, ROWS, RANK), BF16),
            pltpu.VMEM((4, 2, 4, 2, RANK, CH), BF16),
            pltpu.VMEM((4, 3, 4, RANK, CH), BF16),
            pltpu.VMEM((4, 3, 2, RANK, CH), BF16),
            pltpu.VMEM((4, 4, RANK, CH), BF16),
            pltpu.VMEM((4, 2, RANK, CH), BF16),
            pltpu.VMEM((4, 2, 3, RANK, CH), BF16),
            pltpu.VMEM((4, 2, RANK, CH), BF16),
            pltpu.VMEM((2, 2, RANK, CH), BF16),
            dma((6,)),
            dma((4,)),
            dma((4,)),
            dma((3, 2)),
            dma((3, 2)),
            dma((2, 2)),
            dma((4, 2)),
            dma((4, 2, 3)),
            dma((4, 2, 3)),
            dma((4, 2, 3)),
            dma((4, 2, 3)),
            dma((4, 2, 3)),
            dma((4, 2, 3)),
            dma((4, 2, 3)),
            dma((4, 2, 3)),
            dma((4, 2)),
            dma((2, 2)),
            dma((8, 2, 3)),
            dma((8, 2, 3)),
        ],
        compiler_params=pltpu.CompilerParams(
            collective_id=0, has_side_effects=True, vmem_limit_bytes=56 * 2**20
        ),
    )(
        inputs.reshape(ROWS, WIDTH),
        cotangent.reshape(ROWS, WIDTH),
        down_weight[0],
        up_weight[0],
        act_bases.reshape(2, ROWS, WIDTH),
        grad_bases.reshape(2, ROWS, WIDTH),
        gain,
        lim,
        slot,
    )
    return grad_down[None], grad_up[None]


def solution(mesh):
    return jax.shard_map(
        body,
        mesh=mesh,
        in_specs=(
            P(None, "dp", None),
            P(None, "dp", None),
            P("section", "dp", None),
            P("section", "dp", None),
            P("section", None),
            P("section", None, None, "dp", None),
            P("section", None, None, "dp", None),
            P("dp", None),
            P("section", None, "dp", None),
            P("section", None, "dp", None),
        ),
        out_specs=(P("section", "dp", None), P("section", "dp", None)),
        check_vma=False,
    )
```

```python
import functools
import math

import jax
import jax.numpy as jnp
from jax import lax
from jax.experimental import pallas as pl
from jax.experimental.pallas import tpu as pltpu
from jax.sharding import PartitionSpec as P

MESH = pl.DeviceIdType.MESH
F32 = jnp.float32
BF16 = jnp.bfloat16

SECTIONS = 4
WIDTH = 8192
RANK = 128
TOK = 64
ROWS = 2 * TOK
CH = 256
CHUNKS = 8
NORM_EPS = 1e-05
OFF = (1, 3, 2)
DOWN, UP = 0, 1


def dot(a, b):
    return jnp.dot(a, b, preferred_element_type=F32)


def dot_t(a, b):
    return lax.dot_general(a, b, (((1,), (1,)), ((), ())), preferred_element_type=F32)


def kernel(
    x_hbm,
    ct_hbm,
    dw_hbm,
    uw_hbm,
    ab_hbm,
    gb_hbm,
    gain_hbm,
    ae_hbm,
    ge_hbm,
    slot_ref,
    out_ref,
    W,
    acts,
    ups,
    TB,
    GB,
    gain_in,
    exps_in,
    gains,
    lims,
    sel,
    xs,
    xr,
    inner_all,
    inv_all,
    hid_all,
    bis_all,
    G,
    R1d,
    R1u,
    S1d,
    S1u,
    R2,
    S2,
    R3,
    loc_sem,
    base_s,
    base_r,
    small_s,
    small_r,
    p0_s,
    p0_r,
    p1_s,
    p1_r,
    p2_s,
    p2_r,
    r1_s,
    r1_r,
    r2_s,
    r2_r,
    r3_s,
    r3_r,
    x_s,
    x_r,
):
    S, J = lax.axis_index("section"), lax.axis_index("dp")
    xh, c = S // 2, S % 2
    y, xl, z = J // 8, (J // 4) % 2, J % 4
    i_own = z // 2
    src = (z % 2) == c
    not_src = (z % 2) != c

    def dp(yy, xx, zz):
        return yy * 8 + xx * 4 + zz

    def at_y(o):
        return (S, dp((y + o) % 4, xl, z))

    def at_z(o):
        return (S, dp(y, xl, (z + o) % 4))

    def group(e):
        return ((S + e) % 4, J)

    p0_sec = xl * 2 + z % 2

    def p0_dev(xx):
        return (p0_sec, dp(y, xx, z))

    def p0_self(xx):
        return (p0_sec == S) & (xl == xx)

    def owner(s):
        return (s, dp(y, xh, z))

    def owner_self(s):
        return (S == s) & (xl == xh)

    def feat(kk, h, cc):
        return (kk // 2) * 2048 + h * 1024 + ((kk % 2) * 2 + cc) * 256

    def remote(a, b, ss, rs, dev):
        return pltpu.make_async_remote_copy(
            src_ref=a, dst_ref=b, send_sem=ss, recv_sem=rs, device_id=dev, device_id_type=MESH
        )

    def arrived(ref, rs):
        remote(ref, ref, rs, rs, (S, J)).wait_recv()

    def sent(ref, ss):
        remote(ref, ref, ss, ss, (S, J)).wait_send()

    def local_done(ref, sem):
        pltpu.make_async_copy(ref, ref, sem).wait()

    barrier = pltpu.get_barrier_semaphore()

    def greet(dev):
        pl.semaphore_signal(barrier, inc=1, device_id=dev, device_id_type=MESH)

    for e in (1, 2, 3):
        greet(group(e))
        greet(at_y(e))
        greet(at_z(e))
    for xx in (0, 1):
        @pl.when(jnp.logical_not(p0_self(xx)))
        def _():
            greet(p0_dev(xx))
    for s in range(SECTIONS):
        @pl.when(src & jnp.logical_not(owner_self(s)))
        def _():
            greet(owner(s))

    def load(ref_of, dst, sem, h, cc):
        def step(kk, _):
            pltpu.make_async_copy(
                ref_of.at[:, pl.ds(pl.multiple_of(feat(kk, h, cc), 256), CH)], dst.at[kk], sem
            ).start()
            return 0

        lax.fori_loop(0, CHUNKS, step, 0)

    def push(ref_of, dst, ss, rs, h, cc, dev, lo, hi):
        def step(kk, _):
            remote(
                ref_of.at[:, pl.ds(pl.multiple_of(feat(kk, h, cc), 256), CH)],
                dst.at[kk],
                ss,
                rs,
                dev,
            ).start()
            return 0

        lax.fori_loop(lo, hi, step, 0)

    near = 2 * xh
    holds_mid = c != xh
    lacks_mid = c == xh
    cross = (S + 2) % 4
    sib = xh * 2 + (1 - c)

    pltpu.make_async_copy(gain_hbm, gain_in, loc_sem.at[6]).start()
    pltpu.make_async_copy(ae_hbm, exps_in.at[0], loc_sem.at[7]).start()
    pltpu.make_async_copy(ge_hbm, exps_in.at[1], loc_sem.at[8]).start()
    load(x_hbm, acts.at[0], loc_sem.at[0], xh, c)

    is_self0 = jnp.where(p0_self(0) | p0_self(1), 1, 0)
    own_any = jnp.where(xl == xh, 1, 0)
    n_greet = 9 + 2 - is_self0 + jnp.where(src, 4 - own_any, 0)
    pl.semaphore_wait(barrier, n_greet)

    for mat, ref in ((DOWN, dw_hbm), (UP, uw_hbm)):
        for xx in (0, 1):
            there = W.at[S, mat, y, i_own]

            @pl.when(jnp.logical_not(p0_self(xx)))
            def _():
                remote(ref, there, p0_s.at[xx, mat], p0_r.at[S, mat], p0_dev(xx)).start()

            @pl.when(p0_self(xx))
            def _():
                pltpu.make_async_copy(ref, there, p0_r.at[S, mat]).start()

    pltpu.make_async_copy(gain_hbm, gain_in, loc_sem.at[6]).wait()
    gains[S] = gain_in[...].astype(F32)
    pltpu.make_async_copy(ae_hbm, exps_in.at[0], loc_sem.at[7]).wait()
    pltpu.make_async_copy(ge_hbm, exps_in.at[1], loc_sem.at[8]).wait()
    exps = jnp.concatenate([exps_in[0], exps_in[1]], axis=1)
    limit = jnp.full((ROWS, 128), 448.0 * 2.0**-6, F32)
    for e in (7, 8, 9):
        limit = jnp.where(exps == e, 448.0 * 2.0**-e, limit)
    lims[S] = limit.astype(BF16)
    for e in (1, 2, 3):
        remote(gains.at[S], gains.at[S], small_s.at[e - 1, 0], small_r.at[e - 1, 0], group(e)).start()
        remote(lims.at[S], lims.at[S], small_s.at[e - 1, 1], small_r.at[e - 1, 1], group(e)).start()

    def build_sel(kk, _):
        b0 = (kk // 2) * 16 + xh * 8 + (kk % 2) * 4 + c * 2
        row = lax.broadcasted_iota(jnp.int32, (128, CH), 0)
        blk = lax.broadcasted_iota(jnp.int32, (128, CH), 1) // 128 + b0
        sel[0, kk] = jnp.where(row == blk, 1.0, 0.0).astype(BF16)
        sel[1, kk] = jnp.where(row == blk + 64, 1.0, 0.0).astype(BF16)
        return 0

    def t_bases():
        push(ab_hbm.at[1 - c], TB.at[near], base_s.at[0], base_r.at[0], 1 - xh, c, (cross, J), 0, CHUNKS)
        load(ab_hbm.at[1 - c], TB.at[near], loc_sem.at[2], xh, c)

        @pl.when(holds_mid)
        def _():
            push(ab_hbm.at[c], TB.at[1], base_s.at[1], base_r.at[1], xh, 1 - c, (sib, J), 0, CHUNKS)
            load(ab_hbm.at[c], TB.at[1], loc_sem.at[3], xh, c)

    def g_bases():
        load(ct_hbm, ups.at[3], loc_sem.at[1], xh, c)
        load(gb_hbm.at[1 - c], GB.at[near], loc_sem.at[4], xh, c)

        @pl.when(holds_mid)
        def _():
            push(gb_hbm.at[c], GB.at[1], base_s.at[3], base_r.at[3], xh, 1 - c, (sib, J), 0, CHUNKS)
            load(gb_hbm.at[c], GB.at[1], loc_sem.at[5], xh, c)

    def g_cross(lo, hi):
        push(gb_hbm.at[1 - c], GB.at[near], base_s.at[2], base_r.at[2], 1 - xh, c, (cross, J), lo, hi)

    def p0_left():
        for mat, ref in ((DOWN, dw_hbm), (UP, uw_hbm)):
            for xx in (0, 1):
                @pl.when(jnp.logical_not(p0_self(xx)))
                def _():
                    sent(ref, p0_s.at[xx, mat])

    def p1_send(s, mat):
        @pl.when(src)
        def _():
            w = W.at[s, mat, y, i_own]
            arrived(w, p0_r.at[s, mat])
            for d, o in enumerate(OFF):
                there = at_y(o) if mat == DOWN else at_z(o)
                remote(w, w, p1_s.at[s, mat, d], p1_r.at[s, mat, d], there).start()

    def from_z(o):
        return ((z + 4 - o) % 4) // 2

    def z_arrive(view, sems):
        @pl.when(src)
        def _():
            arrived(view(from_z(OFF[2])), sems.at[2])

        @pl.when(not_src)
        def _():
            arrived(view(from_z(OFF[0])), sems.at[0])
            arrived(view(from_z(OFF[1])), sems.at[1])

    def p2_down(s):
        @pl.when(src)
        def _():
            for d, o in enumerate(OFF):
                arrived(W.at[s, DOWN, (y + 4 - o) % 4, i_own], p1_r.at[s, DOWN, d])
            for d, o in enumerate(OFF):
                w = W.at[s, DOWN, :, i_own]
                remote(w, w, p2_s.at[s, DOWN, d], p2_r.at[s, DOWN, d], at_z(o)).start()

    def p2_up(s):
        z_arrive(lambda i: W.at[s, UP, y, i], p1_r.at[s, UP])
        for d, o in enumerate(OFF):
            w = W.at[s, UP, y]
            remote(w, w, p2_s.at[s, UP, d], p2_r.at[s, UP, d], at_y(o)).start()

    def down_ready(s):
        z_arrive(lambda i: W.at[s, DOWN, :, i], p2_r.at[s, DOWN])

    def up_ready(s):
        for d, o in enumerate(OFF):
            arrived(W.at[s, UP, (y + 4 - o) % 4], p2_r.at[s, UP, d])

    def rows(m):
        return pl.ds(m * TOK, TOK)

    def gain_row(s, kk):
        return gains[s, :, pl.ds(pl.multiple_of(feat(kk, xh, c), 256), CH)]

    def fold(v):
        return v[:, :128] + v[:, 128:]

    def chunk_loop(step, init):
        return lax.fori_loop(0, CHUNKS, step, init, unroll=True)

    def x_send(ex, m):
        for e in (1, 2, 3):
            remote(
                xs.at[ex, m], xr.at[ex, m, e - 1], x_s.at[ex, m, e - 1], x_r.at[ex, m, e - 1], group(e)
            ).start()

    def x_total(ex, m, part):
        total = xs[ex, m, part].astype(F32)
        for e in range(3):
            total = total + xr[ex, m, e, part].astype(F32)
        return total

    def x_wait(ex, m):
        for e in range(3):
            arrived(xr.at[ex, m, e], x_r.at[ex, m, e])

    zero = jnp.zeros((TOK, 128), F32)

    def enter(s, kk, value, inner, sq):
        full = value.astype(F32)
        sq = sq + fold(full * full)
        scaled = (full * gain_row(s, kk)).astype(BF16)
        return inner + dot(scaled, W[s, DOWN, kk // 2, kk % 2]), sq

    def hand_over(ex, m, a, b):
        xs[ex, m, 0] = a.astype(BF16)
        xs[ex, m, 1] = b.astype(BF16)
        x_send(ex, m)

    def first(m):
        def step(kk, carry):
            return enter(0, kk, acts[0, kk, rows(m), :], *carry)

        inner, sq = chunk_loop(step, (zero, zero))
        hand_over(0, m, inner, sq)

    def activate(s, m):
        x_wait(s, m)
        mean = jnp.sum(x_total(s, m, 1), axis=-1, keepdims=True) * (1.0 / WIDTH)
        inv = jnp.broadcast_to(lax.rsqrt(mean + NORM_EPS), (TOK, 128))
        inner = x_total(s, m, 0) * inv
        hid = (inner * jax.nn.sigmoid(inner)).astype(BF16)
        inner_all[s, rows(m), :] = inner
        inv_all[s, rows(m), :] = inv
        hid_all[s, rows(m), :] = hid
        return hid

    def recode(value, table, b, m, kk, limit):
        use_first = jnp.full((TOK, CH), slot_ref[0, m]) == 0
        base = jnp.where(
            use_first, table[b, kk, 0:TOK, :].astype(F32), table[b, kk, TOK:ROWS, :].astype(F32)
        )
        delta = jnp.minimum(jnp.maximum(value - base, -limit), limit).astype(BF16)
        return (base + delta.astype(F32)).astype(BF16)

    def forward(s, m):
        hid = activate(s, m)
        table = lims[s, rows(m), :]

        def step(kk, carry):
            out = acts[s, kk, rows(m), :].astype(F32) + dot_t(hid, W[s, UP, kk // 2, kk % 2])
            value = recode(out, TB, s, m, kk, dot(table, sel[0, kk]))
            acts[s + 1, kk, rows(m), :] = value
            return enter(s + 1, kk, value, *carry)

        inner, sq = chunk_loop(step, (zero, zero))
        hand_over(s + 1, m, inner, sq)

    def back_first(m):
        def step(kk, carry):
            return carry + dot(ups[3, kk, rows(m), :], W[3, UP, kk // 2, kk % 2])

        xs[4 + 3, m, 0] = chunk_loop(step, zero).astype(BF16)
        xb_send(3, m)

    def xb_send(s, m):
        for e in (1, 2, 3):
            remote(
                xs.at[4 + s, m, 0],
                xr.at[4 + s, m, e - 1, 0],
                x_s.at[4 + s, m, e - 1],
                x_r.at[4 + s, m, e - 1],
                group(e),
            ).start()

    def back_inner(s, m):
        for e in range(3):
            arrived(xr.at[4 + s, m, e, 0], x_r.at[4 + s, m, e])
        inner, inv = inner_all[s, rows(m), :], inv_all[s, rows(m), :]
        sig = jax.nn.sigmoid(inner)
        bi = x_total(4 + s, m, 0) * sig * (1.0 + inner * (1.0 - sig)) * inv
        bis = bi.astype(BF16)
        bis_all[s, rows(m), :] = bis
        coef = jnp.sum(bis.astype(F32) * inner * inv, axis=-1, keepdims=True) * (1.0 / WIDTH)
        return bis, jnp.broadcast_to(coef, (TOK, CH))

    def backward(s, m):
        bis, coef = back_inner(s, m)
        table = lims[s, rows(m), :]

        def step(kk, carry):
            back = dot_t(bis, W[s, DOWN, kk // 2, kk % 2]) * gain_row(s, kk)
            value = (
                ups[s, kk, rows(m), :].astype(F32)
                + back
                - acts[s, kk, rows(m), :].astype(F32) * coef
            )
            value = recode(value, GB, s - 1, m, kk, dot(table, sel[1, kk]))
            ups[s - 1, kk, rows(m), :] = value
            return carry + dot(value, W[s - 1, UP, kk // 2, kk % 2])

        xs[4 + s - 1, m, 0] = chunk_loop(step, zero).astype(BF16)
        xb_send(s - 1, m)

    def grad_up(s):
        left = jnp.transpose(hid_all[s].astype(F32)).astype(BF16)

        def step(kk, _):
            G[s, UP, kk // 2, kk % 2] = dot(left, ups[s, kk]).astype(BF16)
            return 0

        chunk_loop(step, 0)
        for d, o in enumerate(OFF):
            remote(
                G.at[s, UP, (y + o) % 4], R1u.at[s, d], r1_s.at[s, UP, d], r1_r.at[s, UP, d], at_y(o)
            ).start()

    def to_z(o):
        return ((z + o) % 4) // 2

    def z_give(view, there, ss, rs):
        def give(d):
            o = OFF[d]
            remote(view(to_z(o)), there.at[d], ss.at[d], rs.at[d], at_z(o)).start()

        @pl.when(src)
        def _():
            give(2)

        @pl.when(not_src)
        def _():
            give(0)
            give(1)

    def z_given(view, ss):
        @pl.when(src)
        def _():
            sent(view, ss.at[2])

        @pl.when(not_src)
        def _():
            sent(view, ss.at[0])
            sent(view, ss.at[1])

    def grad_down(s):
        left = jnp.transpose(bis_all[s].astype(F32)).astype(BF16)

        def step(kk, _):
            G[s, DOWN, kk // 2, kk % 2] = (dot(left, acts[s, kk]) * gain_row(s, kk)).astype(BF16)
            return 0

        chunk_loop(step, 0)
        z_give(lambda i: G.at[s, DOWN, :, i], R1d.at[s], r1_s.at[s, DOWN], r1_r.at[s, DOWN])

    def add4(a, b):
        return (
            a.astype(F32) + b[0].astype(F32) + (b[1].astype(F32) + b[2].astype(F32))
        ).astype(BF16)

    def r2_up(s):
        for d in range(3):
            arrived(R1u.at[s, d], r1_r.at[s, UP, d])
        for i in range(2):
            S1u[s, i] = add4(G[s, UP, y, i], [R1u[s, d, i] for d in range(3)])
        z_give(lambda i: S1u.at[s, i], R2.at[s, UP], r2_s.at[s, UP], r2_r.at[s, UP])

    def r2_down(s):
        @pl.when(src)
        def _():
            for d in range(3):
                arrived(R1d.at[s, d], r1_r.at[s, DOWN, d])
            for yy in range(4):
                S1d[s, yy] = add4(G[s, DOWN, yy, i_own], [R1d[s, d, yy] for d in range(3)])
            for d, o in enumerate(OFF):
                remote(
                    S1d.at[s, (y + o) % 4],
                    R2.at[s, DOWN, d],
                    r2_s.at[s, DOWN, d],
                    r2_r.at[s, DOWN, d],
                    at_y(o),
                ).start()

    def r3(s, mat):
        @pl.when(src)
        def _():
            for d in range(3):
                arrived(R2.at[s, mat, d], r2_r.at[s, mat, d])
            own = S1u[s, i_own] if mat == UP else S1d[s, y]
            S2[s, mat] = add4(own, [R2[s, mat, d] for d in range(3)])

            @pl.when(jnp.logical_not(owner_self(s)))
            def _():
                remote(
                    S2.at[s, mat], R3.at[xl, mat], r3_s.at[s, mat], r3_r.at[xl, mat], owner(s)
                ).start()

            @pl.when(owner_self(s))
            def _():
                pltpu.make_async_copy(S2.at[s, mat], R3.at[xl, mat], r3_r.at[xl, mat]).start()

    def base_ready(table, b, near_sem, mid_sem, far_sem, mid_far_sem):
        if b == 1:
            @pl.when(holds_mid)
            def _():
                local_done(table.at[1], mid_sem)

            @pl.when(lacks_mid)
            def _():
                arrived(table.at[1], mid_far_sem)
        else:
            @pl.when(near == b)
            def _():
                local_done(table.at[b], near_sem)

            @pl.when(near != b)
            def _():
                arrived(table.at[b], far_sem)

    lax.fori_loop(0, CHUNKS, build_sel, 0)
    for mat in (DOWN, UP):
        for s in (0, 1):
            p1_send(s, mat)
    p0_left()
    t_bases()
    p2_down(0)
    for s in (2, 3):
        for mat in (DOWN, UP):
            p1_send(s, mat)
    g_bases()
    p2_up(0)
    for s in (1, 2, 3):
        p2_down(s)
        p2_up(s)
    for e in (1, 2, 3):
        arrived(gains.at[(S + 4 - e) % 4], small_r.at[e - 1, 0])
        arrived(lims.at[(S + 4 - e) % 4], small_r.at[e - 1, 1])
    local_done(acts.at[0], loc_sem.at[0])
    down_ready(0)
    first(0)
    first(1)
    g_cross(0, 3)
    for s in range(SECTIONS - 1):
        up_ready(s)
        base_ready(TB, s, loc_sem.at[2], loc_sem.at[3], base_r.at[0], base_r.at[1])
        down_ready(s + 1)
        forward(s, 0)
        forward(s, 1)
        if s < 2:
            g_cross(3 * s + 3, min(3 * s + 6, CHUNKS))
    up_ready(3)
    local_done(ups.at[3], loc_sem.at[1])
    back_first(0)
    back_first(1)
    activate(3, 0)
    activate(3, 1)
    grad_up(3)
    for s in (3, 2, 1):
        base_ready(GB, s - 1, loc_sem.at[4], loc_sem.at[5], base_r.at[2], base_r.at[3])
        backward(s, 0)
        backward(s, 1)
        grad_down(s)
        grad_up(s - 1)
    r2_up(3)
    back_inner(0, 0)
    back_inner(0, 1)
    grad_down(0)
    r2_down(3)
    for s in (2, 1, 0):
        r2_up(s)
        r2_down(s)
    for s in (3, 2, 1, 0):
        r3(s, UP)
        r3(s, DOWN)

    scale = 1.0 / math.sqrt(2 * 2048)
    for mat in (UP, DOWN):
        for xx in (0, 1):
            arrived(R3.at[xx, mat], r3_r.at[xx, mat])
        total = (R3[0, mat].astype(F32) + R3[1, mat].astype(F32)) * scale
        out_ref[mat] = jnp.transpose(total)

    for e in range(3):
        sent(gains.at[0], small_s.at[e, 0])
        sent(lims.at[0], small_s.at[e, 1])
    sent(TB.at[0], base_s.at[0])
    sent(GB.at[0], base_s.at[2])

    @pl.when(holds_mid)
    def _():
        sent(TB.at[1], base_s.at[1])
        sent(GB.at[1], base_s.at[3])

    def drain(s, _):
        @pl.when(src)
        def _():
            for d in range(3):
                sent(W.at[s, DOWN, y, i_own], p1_s.at[s, DOWN, d])
                sent(W.at[s, UP, y, i_own], p1_s.at[s, UP, d])
                sent(W.at[s, DOWN, :, i_own], p2_s.at[s, DOWN, d])
                sent(S1d.at[s, 0], r2_s.at[s, DOWN, d])

            @pl.when(jnp.logical_not(owner_self(s)))
            def _():
                for mat in (DOWN, UP):
                    sent(S2.at[s, mat], r3_s.at[s, mat])

        for d in range(3):
            sent(W.at[s, UP, y], p2_s.at[s, UP, d])
            sent(G.at[s, UP, 0], r1_s.at[s, UP, d])
        z_given(G.at[s, DOWN, :, 0], r1_s.at[s, DOWN])
        z_given(S1u.at[s, 0], r2_s.at[s, UP])
        for m in (0, 1):
            for e in range(3):
                sent(xs.at[s, m], x_s.at[s, m, e])
                sent(xs.at[4 + s, m, 0], x_s.at[4 + s, m, e])
        return 0

    lax.fori_loop(0, SECTIONS, drain, 0)


def split(both_ref, down_ref, up_ref):
    down_ref[0] = both_ref[DOWN]
    up_ref[0] = both_ref[UP]


def body(
    inputs,
    cotangent,
    down_weight,
    up_weight,
    section_gains,
    act_bases,
    grad_bases,
    slot_ids,
    act_exps,
    grad_exps,
):
    any_spec = pl.BlockSpec(memory_space=pl.ANY)
    vmem = pl.BlockSpec(memory_space=pltpu.VMEM)
    dma = pltpu.SemaphoreType.DMA
    both = pl.pallas_call(
        kernel,
        out_shape=jax.ShapeDtypeStruct((2, CH, RANK), F32),
        in_specs=[any_spec] * 9 + [pl.BlockSpec(memory_space=pltpu.SMEM)],
        out_specs=vmem,
        scratch_shapes=[
            pltpu.VMEM((4, 2, 4, 2, CH, RANK), BF16),
            pltpu.VMEM((4, CHUNKS, ROWS, CH), BF16),
            pltpu.VMEM((4, CHUNKS, ROWS, CH), BF16),
            pltpu.VMEM((3, CHUNKS, ROWS, CH), BF16),
            pltpu.VMEM((3, CHUNKS, ROWS, CH), BF16),
            pltpu.VMEM((1, WIDTH), BF16),
            pltpu.VMEM((2, ROWS, 64), jnp.int32),
            pltpu.VMEM((4, 1, WIDTH), F32),
            pltpu.VMEM((4, ROWS, 128), BF16),
            pltpu.VMEM((2, CHUNKS, 128, CH), BF16),
            pltpu.VMEM((8, 2, 2, TOK, 128), BF16),
            pltpu.VMEM((8, 2, 3, 2, TOK, 128), BF16),
            pltpu.VMEM((4, ROWS, RANK), F32),
            pltpu.VMEM((4, ROWS, RANK), F32),
            pltpu.VMEM((4, ROWS, RANK), BF16),
            pltpu.VMEM((4, ROWS, RANK), BF16),
            pltpu.VMEM((4, 2, 4, 2, RANK, CH), BF16),
            pltpu.VMEM((4, 3, 4, RANK, CH), BF16),
            pltpu.VMEM((4, 3, 2, RANK, CH), BF16),
            pltpu.VMEM((4, 4, RANK, CH), BF16),
            pltpu.VMEM((4, 2, RANK, CH), BF16),
            pltpu.VMEM((4, 2, 3, RANK, CH), BF16),
            pltpu.VMEM((4, 2, RANK, CH), BF16),
            pltpu.VMEM((2, 2, RANK, CH), BF16),
            dma((9,)),
            dma((4,)),
            dma((4,)),
            dma((3, 2)),
            dma((3, 2)),
            dma((2, 2)),
            dma((4, 2)),
            dma((4, 2, 3)),
            dma((4, 2, 3)),
            dma((4, 2, 3)),
            dma((4, 2, 3)),
            dma((4, 2, 3)),
            dma((4, 2, 3)),
            dma((4, 2, 3)),
            dma((4, 2, 3)),
            dma((4, 2)),
            dma((2, 2)),
            dma((8, 2, 3)),
            dma((8, 2, 3)),
        ],
        compiler_params=pltpu.CompilerParams(
            collective_id=0, has_side_effects=True, vmem_limit_bytes=56 * 2**20
        ),
    )(
        inputs.reshape(ROWS, WIDTH),
        cotangent.reshape(ROWS, WIDTH),
        down_weight[0],
        up_weight[0],
        act_bases.reshape(2, ROWS, WIDTH),
        grad_bases.reshape(2, ROWS, WIDTH),
        section_gains,
        act_exps.reshape(ROWS, 64),
        grad_exps.reshape(ROWS, 64),
        slot_ids,
    )
    grad_down, grad_up = pl.pallas_call(
        split,
        out_shape=(jax.ShapeDtypeStruct((1, CH, RANK), F32),) * 2,
        in_specs=[vmem],
        out_specs=(vmem, vmem),
    )(both)
    return grad_down, grad_up


def solution(mesh):
    return jax.shard_map(
        body,
        mesh=mesh,
        in_specs=(
            P(None, "dp", None),
            P(None, "dp", None),
            P("section", "dp", None),
            P("section", "dp", None),
            P("section", None),
            P("section", None, None, "dp", None),
            P("section", None, None, "dp", None),
            P("dp", None),
            P("section", None, "dp", None),
            P("section", None, "dp", None),
        ),
        out_specs=(P("section", "dp", None), P("section", "dp", None)),
        check_vma=False,
    )
```

```python
import functools
import math

import jax
import jax.numpy as jnp
from jax import lax
from jax.experimental import pallas as pl
from jax.experimental.pallas import tpu as pltpu
from jax.sharding import PartitionSpec as P

MESH = pl.DeviceIdType.MESH
F32 = jnp.float32
BF16 = jnp.bfloat16

SECTIONS = 4
WIDTH = 8192
RANK = 128
TOK = 64
ROWS = 2 * TOK
CH = 256
CHUNKS = 8
NORM_EPS = 1e-05
OFF = (1, 3, 2)
DOWN, UP = 0, 1
(
    L_P0,
    L_GAIN,
    L_LIM,
    L_BASE,
    L_W1,
    L_W0,
    L_WD,
    L_WU,
    L_RU,
    L_RD,
    L_RA,
    L_RB,
    L_R2U,
    L_R2D,
    L_R2L,
    L_R3,
    L_X,
    LEFT_KINDS,
) = range(18)


def dot(a, b):
    return jnp.dot(a, b, preferred_element_type=F32)


def dot_t(a, b):
    return lax.dot_general(a, b, (((1,), (1,)), ((), ())), preferred_element_type=F32)


def kernel(
    x_hbm,
    ct_hbm,
    dw_hbm,
    uw_hbm,
    ab_hbm,
    gb_hbm,
    gain_hbm,
    ae_hbm,
    ge_hbm,
    slot_ref,
    out_ref,
    W,
    acts,
    ups,
    TB,
    GB,
    gain_in,
    exps_in,
    gains,
    lims,
    sel,
    xs,
    xr,
    inner_all,
    inv_all,
    hid_all,
    bis_all,
    G,
    R1d,
    R1u,
    S1d,
    S1u,
    R2,
    S2,
    R3,
    R1h,
    S1h,
    Qd,
    Qu,
    LX,
    wide,
    narrow,
    loc_sem,
    t_ready,
    g_ready,
    gain_r,
    lim_r,
    p0_r,
    p1_r,
    h1_r,
    h2_r,
    p2_r,
    p2b_r,
    q_r,
    r1_r,
    g1_r,
    r2_r,
    r3_r,
    x_r,
    left,
):
    S, J = lax.axis_index("section"), lax.axis_index("dp")
    xh, c = S // 2, S % 2
    y, xl, z = J // 8, (J // 4) % 2, J % 4
    i_own = z // 2
    src = (z % 2) == c
    not_src = (z % 2) != c

    def dp(yy, xx, zz):
        return yy * 8 + xx * 4 + zz

    def at_y(o):
        return (S, dp((y + o) % 4, xl, z))

    def at_z(o):
        return (S, dp(y, xl, (z + o) % 4))

    def group(e):
        return ((S + e) % 4, J)

    p0_sec = xl * 2 + z % 2

    def p0_dev(xx):
        return (p0_sec, dp(y, xx, z))

    def p0_self(xx):
        return (p0_sec == S) & (xl == xx)

    def owner(s):
        return (s, dp(y, xh, z))

    def owner_self(s):
        return (S == s) & (xl == xh)

    def feat(kk, h, cc):
        return (kk // 2) * 2048 + h * 1024 + ((kk % 2) * 2 + cc) * 256

    def remote(a, b, ss, rs, dev):
        return pltpu.make_async_remote_copy(
            src_ref=a, dst_ref=b, send_sem=ss, recv_sem=rs, device_id=dev, device_id_type=MESH
        )

    def arrived(ref, rs):
        remote(ref, ref, rs, rs, (S, J)).wait_recv()

    def sent(ref, ss):
        remote(ref, ref, ss, ss, (S, J)).wait_send()

    def local_done(ref, sem):
        pltpu.make_async_copy(ref, ref, sem).wait()

    barrier = pltpu.get_barrier_semaphore()

    def greet(dev):
        pl.semaphore_signal(barrier, inc=1, device_id=dev, device_id_type=MESH)

    for e in (1, 2, 3):
        greet(group(e))
        greet(at_y(e))
        greet(at_z(e))
    for xx in (0, 1):
        @pl.when(jnp.logical_not(p0_self(xx)))
        def _():
            greet(p0_dev(xx))
    for s in range(SECTIONS):
        @pl.when(src & jnp.logical_not(owner_self(s)))
        def _():
            greet(owner(s))

    def load(ref_of, dst, sem, h, cc):
        def step(kk, _):
            pltpu.make_async_copy(
                ref_of.at[:, pl.ds(pl.multiple_of(feat(kk, h, cc), 256), CH)], dst.at[kk], sem
            ).start()
            return 0

        lax.fori_loop(0, CHUNKS, step, 0)

    def push(ref_of, dst, ss, rs, h, cc, dev, lo, hi):
        def step(kk, _):
            remote(
                ref_of.at[:, pl.ds(pl.multiple_of(feat(kk, h, cc), 256), CH)],
                dst.at[kk],
                ss,
                rs,
                dev,
            ).start()
            return 0

        lax.fori_loop(lo, hi, step, 0)

    near = 2 * xh
    holds_mid = c != xh
    lacks_mid = c == xh
    cross = (S + 2) % 4
    sib = xh * 2 + (1 - c)

    pltpu.make_async_copy(gain_hbm, gain_in, loc_sem.at[2]).start()
    pltpu.make_async_copy(ae_hbm, exps_in.at[0], loc_sem.at[3]).start()
    pltpu.make_async_copy(ge_hbm, exps_in.at[1], loc_sem.at[3]).start()
    load(x_hbm, acts.at[0], loc_sem.at[0], xh, c)

    is_self0 = jnp.where(p0_self(0) | p0_self(1), 1, 0)
    own_any = jnp.where(xl == xh, 1, 0)
    n_greet = 9 + 2 - is_self0 + jnp.where(src, 4 - own_any, 0)
    pl.semaphore_wait(barrier, n_greet)

    def p0_send():
        for mat, ref in ((DOWN, dw_hbm), (UP, uw_hbm)):
            for xx in (0, 1):
                there = W.at[S, mat, y, i_own]

                @pl.when(jnp.logical_not(p0_self(xx)))
                def _():
                    remote(ref, there, left.at[L_P0], p0_r.at[S, mat], p0_dev(xx)).start()

                @pl.when(p0_self(xx))
                def _():
                    pltpu.make_async_copy(ref, there, p0_r.at[S, mat]).start()

    pl.when(c == 0)(p0_send)

    pltpu.make_async_copy(gain_hbm, gain_in, loc_sem.at[2]).wait()
    gains[S] = gain_in[...].astype(F32)
    local_done(exps_in, loc_sem.at[3])
    exps = jnp.concatenate([exps_in[0], exps_in[1]], axis=1)
    limit = jnp.full((ROWS, 128), 448.0 * 2.0**-6, F32)
    for e in (7, 8, 9):
        limit = jnp.where(exps == e, 448.0 * 2.0**-e, limit)
    lims[S] = limit.astype(BF16)
    pl.when(c == 1)(p0_send)
    for e in (1, 2, 3):
        remote(gains.at[S], gains.at[S], left.at[L_GAIN], gain_r.at[0], group(e)).start()
        remote(lims.at[S], lims.at[S], left.at[L_LIM], lim_r.at[0], group(e)).start()

    def build_sel(kk, _):
        b0 = (kk // 2) * 16 + xh * 8 + (kk % 2) * 4 + c * 2
        row = lax.broadcasted_iota(jnp.int32, (128, CH), 0)
        blk = lax.broadcasted_iota(jnp.int32, (128, CH), 1) // 128 + b0
        sel[0, kk] = jnp.where(row == blk, 1.0, 0.0).astype(BF16)
        sel[1, kk] = jnp.where(row == blk + 64, 1.0, 0.0).astype(BF16)
        return 0

    def t_bases():
        push(ab_hbm.at[1 - c], TB.at[near], left.at[L_BASE], t_ready.at[near], 1 - xh, c, (cross, J), 0, CHUNKS)
        load(ab_hbm.at[1 - c], TB.at[near], t_ready.at[near], xh, c)

        @pl.when(holds_mid)
        def _():
            push(ab_hbm.at[c], TB.at[1], left.at[L_BASE], t_ready.at[1], xh, 1 - c, (sib, J), 0, CHUNKS)
            load(ab_hbm.at[c], TB.at[1], t_ready.at[1], xh, c)

    def g_bases():
        load(ct_hbm, ups.at[3], loc_sem.at[1], xh, c)
        load(gb_hbm.at[1 - c], GB.at[near], g_ready.at[near], xh, c)

        @pl.when(holds_mid)
        def _():
            push(gb_hbm.at[c], GB.at[1], left.at[L_BASE], g_ready.at[1], xh, 1 - c, (sib, J), 0, CHUNKS)
            load(gb_hbm.at[c], GB.at[1], g_ready.at[1], xh, c)

    def g_cross(lo, hi):
        push(gb_hbm.at[1 - c], GB.at[near], left.at[L_BASE], g_ready.at[near], 1 - xh, c, (cross, J), lo, hi)

    def p0_left():
        keeps = p0_self(0) | p0_self(1)

        @pl.when(keeps)
        def _():
            sent(W.at[0, 0, 0], left.at[L_P0])

        @pl.when(jnp.logical_not(keeps))
        def _():
            sent(W.at[0, 0, 0:2], left.at[L_P0])

    half = CH // 2
    low, high = pl.ds(0, half), pl.ds(half, half)
    SIDES = ((0, 1), (1, 3))

    def z_take(one, two, sem):
        pl.when(src)(lambda: arrived(one, sem))
        pl.when(not_src)(lambda: arrived(two, sem))

    def p1_send(s, mat):
        @pl.when(src)
        def _():
            w = W.at[s, mat, y, i_own]
            arrived(w, p0_r.at[s, mat])
            for o in OFF:
                there = at_y(o) if mat == DOWN else at_z(o)
                remote(w, w, left.at[L_W1], p1_r.at[s, mat], there).start()

    def p1_first():
        @pl.when(src)
        def _():
            w = W.at[0, DOWN, y, i_own]
            arrived(w, p0_r.at[0, DOWN])
            for o in OFF:
                v = w.at[low]
                remote(v, v, left.at[L_W1], p1_r.at[0, DOWN], at_y(o)).start()
                v = w.at[high]
                remote(v, v, left.at[L_W1], h1_r.at[0], at_z(o)).start()

    def p2_first():
        @pl.when(src)
        def _():
            arrived(W.at[0, DOWN, 0:3, 0, low], p1_r.at[0, DOWN])
            for o in OFF:
                w = W.at[0, DOWN, :, i_own, low]
                remote(w, w, left.at[L_W0], p2_r.at[0, DOWN], at_z(o)).start()

        z_take(W.at[0, DOWN, 0, 0, high], W.at[0, DOWN, 0, :, high], h1_r.at[0])
        for o in OFF:
            w = W.at[0, DOWN, y, :, high]
            remote(w, w, left.at[L_W0], h2_r.at[0], at_y(o)).start()

    def first_ready():
        z_take(W.at[0, DOWN, :, 0, low], W.at[0, DOWN, :, :, low], p2_r.at[0, DOWN])
        arrived(W.at[0, DOWN, 0:3, :, high], h2_r.at[0])

    def p2_down(s):
        @pl.when(src)
        def _():
            arrived(W.at[s, DOWN, 0:3, 0], p1_r.at[s, DOWN])
            for o in (1, 3):
                w = W.at[s, DOWN, :, i_own]
                remote(w, w, left.at[L_WD], p2_r.at[s, DOWN], at_z(o)).start()

    def p3_down(s):
        @pl.when(not_src)
        def _():
            arrived(W.at[s, DOWN], p2_r.at[s, DOWN])
            for d, o in SIDES:
                w = W.at[s, DOWN, pair(d), ((z + 4 - o) % 4) // 2]
                remote(w, w, left.at[L_WD], p2_r.at[s, DOWN], at_z(o)).start()

    def down_ready(s):
        pl.when(src)(lambda: arrived(W.at[s, DOWN, :, 0], p2_r.at[s, DOWN]))

    def p2_up(s):
        z_take(W.at[s, UP, 0, 0], W.at[s, UP, 0], p1_r.at[s, UP])
        for o in OFF if s == 0 else (1, 3):
            w = W.at[s, UP, y]
            remote(w, w, left.at[L_WU], p2_r.at[s, UP], at_y(o)).start()

    def p3_up(s):
        arrived(W.at[s, UP, 0:2], p2_r.at[s, UP])
        for d, o in SIDES:
            w = W.at[s, UP, (y + 4 - o) % 4, d]
            remote(w, w, left.at[L_WU], p2b_r.at[s], at_y(o)).start()

    def up_ready(s):
        if s == 0:
            arrived(W.at[s, UP, 0:3], p2_r.at[s, UP])
        else:
            arrived(W.at[s, UP, 0], p2b_r.at[s])

    def pair(d):
        return pl.ds(2 * d, 2)

    def rows(m):
        return pl.ds(m * TOK, TOK)

    def gain_row(s, kk):
        return gains[s, :, pl.ds(pl.multiple_of(feat(kk, xh, c), 256), CH)]

    def fold(v):
        return v[:, :128] + v[:, 128:]

    def chunk_loop(step, init):
        return lax.fori_loop(0, CHUNKS, step, init, unroll=True)

    def x_send(ex, m):
        for e in (1, 2, 3):
            remote(
                xs.at[ex, m], xr.at[ex, m, e - 1], left.at[L_X], x_r.at[ex, m], group(e)
            ).start()

    def x_total(ex, m, part):
        total = xs[ex, m, part].astype(F32)
        for e in range(3):
            total = total + xr[ex, m, e, part].astype(F32)
        return total

    def x_wait(ex, m):
        arrived(xr.at[ex, m], x_r.at[ex, m])

    zero = jnp.zeros((TOK, 128), F32)

    def enter(s, kk, value, inner, sq):
        full = value.astype(F32)
        sq = sq + fold(full * full)
        scaled = (full * gain_row(s, kk)).astype(BF16)
        return inner + dot(scaled, W[s, DOWN, kk // 2, kk % 2]), sq

    def hand_over(ex, m, a, b):
        xs[ex, m, 0] = a.astype(BF16)
        xs[ex, m, 1] = b.astype(BF16)
        x_send(ex, m)

    def first(m):
        def step(kk, carry):
            return enter(0, kk, acts[0, kk, rows(m), :], *carry)

        inner, sq = chunk_loop(step, (zero, zero))
        hand_over(0, m, inner, sq)

    def activate(s, m):
        x_wait(s, m)
        mean = jnp.sum(x_total(s, m, 1), axis=-1, keepdims=True) * (1.0 / WIDTH)
        inv = jnp.broadcast_to(lax.rsqrt(mean + NORM_EPS), (TOK, 128))
        inner = x_total(s, m, 0) * inv
        hid = (inner * jax.nn.sigmoid(inner)).astype(BF16)
        inner_all[s, rows(m), :] = inner
        inv_all[s, rows(m), :] = inv
        hid_all[s, rows(m), :] = hid
        return hid

    def spread(t, s):
        def step(kk, _):
            LX[t, s - t, kk] = dot(lims[s], sel[t, kk]).astype(BF16)
            return 0

        chunk_loop(step, 0)

    def order(table, b):
        straight = jnp.full((TOK, CH), slot_ref[0, 0]) == 0

        def step(kk, _):
            one = table[b, kk, 0:TOK, :].astype(F32)
            two = table[b, kk, TOK:ROWS, :].astype(F32)
            table[b, kk, 0:TOK, :] = jnp.where(straight, one, two).astype(BF16)
            table[b, kk, TOK:ROWS, :] = jnp.where(straight, two, one).astype(BF16)
            return 0

        chunk_loop(step, 0)

    def recode(value, base, limit):
        base, limit = base.astype(F32), limit.astype(F32)
        delta = jnp.minimum(jnp.maximum(value - base, -limit), limit).astype(BF16)
        return (base + delta.astype(F32)).astype(BF16)

    def cols(kk):
        return pl.ds(pl.multiple_of(kk * CH, CH), CH)

    def flat(s, mat):
        return W[s, mat].reshape(CHUNKS * CH, RANK)

    def forward(s, m):
        hid = activate(s, m)
        wide[...] = dot_t(hid, flat(s, UP))

        def step(kk, sq):
            out = acts[s, kk, rows(m), :].astype(F32) + wide[:, cols(kk)]
            value = recode(out, TB[s, kk, rows(m), :], LX[0, s, kk, rows(m), :])
            acts[s + 1, kk, rows(m), :] = value
            full = value.astype(F32)
            narrow[:, cols(kk)] = (full * gain_row(s + 1, kk)).astype(BF16)
            return sq + fold(full * full)

        sq = chunk_loop(step, zero)
        hand_over(s + 1, m, dot(narrow[...], flat(s + 1, DOWN)), sq)

    def back_first(m):
        def step(kk, carry):
            return carry + dot(ups[3, kk, rows(m), :], W[3, UP, kk // 2, kk % 2])

        xs[4 + 3, m, 0] = chunk_loop(step, zero).astype(BF16)
        xb_send(3, m)

    def xb_send(s, m):
        for e in (1, 2, 3):
            remote(
                xs.at[4 + s, m, 0],
                xr.at[4 + s, m, e - 1, 0],
                left.at[L_X],
                x_r.at[4 + s, m],
                group(e),
            ).start()

    def back_inner(s, m):
        arrived(xr.at[4 + s, m, :, 0], x_r.at[4 + s, m])
        inner, inv = inner_all[s, rows(m), :], inv_all[s, rows(m), :]
        sig = jax.nn.sigmoid(inner)
        bi = x_total(4 + s, m, 0) * sig * (1.0 + inner * (1.0 - sig)) * inv
        bis = bi.astype(BF16)
        bis_all[s, rows(m), :] = bis
        coef = jnp.sum(bis.astype(F32) * inner * inv, axis=-1, keepdims=True) * (1.0 / WIDTH)
        return bis, jnp.broadcast_to(coef, (TOK, CH))

    def backward(s, m):
        bis, coef = back_inner(s, m)
        wide[...] = dot_t(bis, flat(s, DOWN))

        def step(kk, _):
            value = (
                ups[s, kk, rows(m), :].astype(F32)
                + wide[:, cols(kk)] * gain_row(s, kk)
                - acts[s, kk, rows(m), :].astype(F32) * coef
            )
            value = recode(value, GB[s - 1, kk, rows(m), :], LX[1, s - 1, kk, rows(m), :])
            ups[s - 1, kk, rows(m), :] = value
            narrow[:, cols(kk)] = value
            return 0

        chunk_loop(step, 0)
        xs[4 + s - 1, m, 0] = dot(narrow[...], flat(s - 1, UP)).astype(BF16)
        xb_send(s - 1, m)

    def make_grad_up(s):
        left = jnp.transpose(hid_all[s].astype(F32)).astype(BF16)

        def step(kk, _):
            G[s, UP, kk // 2, kk % 2] = dot(left, ups[s, kk]).astype(BF16)
            return 0

        chunk_loop(step, 0)

    def make_grad_down(s):
        left = jnp.transpose(bis_all[s].astype(F32)).astype(BF16)

        def step(kk, _):
            G[s, DOWN, kk // 2, kk % 2] = (dot(left, acts[s, kk]) * gain_row(s, kk)).astype(BF16)
            return 0

        chunk_loop(step, 0)

    def to_z(o):
        return ((z + o) % 4) // 2

    def z_give(view, there, kind, rs):
        def give(d):
            o = OFF[d]
            remote(view(to_z(o)), there.at[d], left.at[kind], rs, at_z(o)).start()

        @pl.when(src)
        def _():
            give(2)

        @pl.when(not_src)
        def _():
            give(0)
            give(1)

    rlow, rhigh = pl.ds(0, RANK // 2), pl.ds(RANK // 2, RANK // 2)

    def grad_down_last():
        make_grad_down(0)
        z_give(lambda i: G.at[0, DOWN, :, i, rlow], R1d.at[0, :, :, rlow], L_RA, r1_r.at[0, DOWN])
        for d, o in enumerate(OFF):
            remote(G.at[0, DOWN, (y + o) % 4, :, rhigh], R1h.at[d], left.at[L_RB], g1_r.at[0], at_y(o)).start()

    def send_grad_up(s):
        for d, o in SIDES:
            remote(G.at[s, UP, (y + 2) % 4, d], Qu.at[s, d], left.at[L_RU], q_r.at[s, UP], at_y(o)).start()
        for d, o in SIDES:
            remote(
                G.at[s, UP, (y + o) % 4, 1 - d], R1u.at[s, d, 1 - d], left.at[L_RU], r1_r.at[s, UP], at_y(o)
            ).start()

    def relay_up(s):
        arrived(Qu.at[s], q_r.at[s, UP])
        for d, o in SIDES:
            own = G[s, UP, (y + o) % 4, d].astype(F32)
            G[s, UP, (y + o) % 4, d] = (own + Qu[s, d].astype(F32)).astype(BF16)
            remote(
                G.at[s, UP, (y + o) % 4, d], R1u.at[s, d, d], left.at[L_RU], r1_r.at[s, UP], at_y(o)
            ).start()

    def send_grad_down(s):
        @pl.when(src)
        def _():
            for d, o in SIDES:
                remote(
                    G.at[s, DOWN, pair(d), 1 - i_own], Qd.at[s, d], left.at[L_RD], q_r.at[s, DOWN], at_z(o)
                ).start()

        @pl.when(not_src)
        def _():
            for d, o in SIDES:
                remote(
                    G.at[s, DOWN, pair(1 - d), to_z(o)],
                    R1d.at[s, d, pair(1 - d)],
                    left.at[L_RD],
                    r1_r.at[s, DOWN],
                    at_z(o),
                ).start()

    def relay_down(s):
        @pl.when(not_src)
        def _():
            arrived(Qd.at[s], q_r.at[s, DOWN])
            for d, o in SIDES:
                for k in range(2):
                    own = G[s, DOWN, 2 * d + k, to_z(o)].astype(F32)
                    G[s, DOWN, 2 * d + k, to_z(o)] = (own + Qd[s, d, k].astype(F32)).astype(BF16)
                remote(
                    G.at[s, DOWN, pair(d), to_z(o)],
                    R1d.at[s, d, pair(d)],
                    left.at[L_RD],
                    r1_r.at[s, DOWN],
                    at_z(o),
                ).start()

    def add_up(a, parts):
        total = a.astype(F32)
        for part in parts:
            total = total + part.astype(F32)
        return total.astype(BF16)

    def r2_up(s):
        arrived(R1u.at[s], r1_r.at[s, UP])
        for i in range(2):
            S1u[s, i] = add_up(G[s, UP, y, i], [R1u[s, d, i] for d in range(2)])
        z_give(lambda i: S1u.at[s, i], R2.at[s, UP], L_R2U, r2_r.at[s, UP])

    def r2_down(s):
        @pl.when(src)
        def _():
            arrived(R1d.at[s, 0:2], r1_r.at[s, DOWN])
            for yy in range(4):
                S1d[s, yy] = add_up(G[s, DOWN, yy, i_own], [R1d[s, d, yy] for d in range(2)])
            for d, o in enumerate(OFF):
                remote(
                    S1d.at[s, (y + o) % 4], R2.at[s, DOWN, d], left.at[L_R2D], r2_r.at[s, DOWN], at_y(o)
                ).start()

    def r2_last():
        @pl.when(src)
        def _():
            arrived(R1d.at[0, :, :, rlow], r1_r.at[0, DOWN])
            for yy in range(4):
                S1d[0, yy, rlow, :] = add_up(
                    G[0, DOWN, yy, i_own, rlow, :], [R1d[0, d, yy, rlow, :] for d in range(3)]
                )
            for d, o in enumerate(OFF):
                remote(
                    S1d.at[0, (y + o) % 4, rlow],
                    R2.at[0, DOWN, d, rlow],
                    left.at[L_R2L],
                    r2_r.at[0, DOWN],
                    at_y(o),
                ).start()

        arrived(R1h, g1_r.at[0])
        for i in range(2):
            S1h[i] = add_up(G[0, DOWN, y, i, rhigh, :], [R1h[d, i] for d in range(3)])
        z_give(lambda i: S1h.at[i], R2.at[0, DOWN, :, rhigh], L_R2L, r2_r.at[0, DOWN])

    def r3(s, mat):
        @pl.when(src)
        def _():
            arrived(R2.at[s, mat], r2_r.at[s, mat])
            if s == 0 and mat == DOWN:
                for part, own in ((rlow, S1d[s, y, rlow, :]), (rhigh, S1h[i_own])):
                    S2[s, mat, part, :] = add_up(own, [R2[s, mat, d, part, :] for d in range(3)])
            else:
                own = S1u[s, i_own] if mat == UP else S1d[s, y]
                S2[s, mat] = add_up(own, [R2[s, mat, d] for d in range(3)])

            @pl.when(jnp.logical_not(owner_self(s)))
            def _():
                remote(S2.at[s, mat], R3.at[xl, mat], left.at[L_R3], r3_r.at[mat], owner(s)).start()

            @pl.when(owner_self(s))
            def _():
                pltpu.make_async_copy(S2.at[s, mat], R3.at[xl, mat], r3_r.at[mat]).start()

    def base_ready(table, b, sems):
        arrived(table.at[b], sems.at[b])

    def drain():
        sent(gains.at[0:3], left.at[L_GAIN])
        sent(lims.at[0:3], left.at[L_LIM])
        pl.when(holds_mid)(lambda: sent(acts, left.at[L_BASE]))
        pl.when(lacks_mid)(lambda: sent(TB.at[0:2], left.at[L_BASE]))
        pl.when(src)(lambda: sent(W.at[0:3, 0], left.at[L_W1]))
        pl.when(src)(lambda: sent(R2.at[0:3, 0], left.at[L_W0]))
        pl.when(not_src)(lambda: sent(R2.at[0, 0], left.at[L_W0]))
        pl.when(src)(lambda: sent(W.at[0:3, 0], left.at[L_WD]))
        pl.when(not_src)(lambda: sent(W.at[0:3, 0, 0:2], left.at[L_WD]))
        sent(W.at[0:3, 0], left.at[L_WU])
        sent(W.at[0:3, 0], left.at[L_RU])
        pl.when(src)(lambda: sent(W.at[0:3, 0, 0:2], left.at[L_RD]))
        pl.when(not_src)(lambda: sent(W.at[0:3, 0], left.at[L_RD]))
        pl.when(src)(lambda: sent(W.at[0, 0, 0], left.at[L_RA]))
        pl.when(not_src)(lambda: sent(W.at[0, 0, 0:2], left.at[L_RA]))
        sent(R1h, left.at[L_RB])
        pl.when(src)(lambda: sent(W.at[0, 0, 0:2], left.at[L_R2U]))
        pl.when(not_src)(lambda: sent(W.at[0, 0], left.at[L_R2U]))
        pl.when(src)(lambda: sent(R2.at[0:3, 0], left.at[L_R2D]))
        pl.when(src)(lambda: sent(W.at[0, 0, 0], left.at[L_R2L]))
        pl.when(not_src)(lambda: sent(W.at[0, 0, 0, 0], left.at[L_R2L]))
        sent(xr.at[0:6], left.at[L_X])

    lax.fori_loop(0, CHUNKS, build_sel, 0)

    def p1_late():
        for mat in (DOWN, UP):
            for s in (2, 3):
                p1_send(s, mat)

    pl.when(xh == 1)(p1_late)
    p1_first()
    p1_send(1, DOWN)
    p1_send(0, UP)
    p1_send(1, UP)
    p0_left()
    t_bases()
    pl.when(xh == 0)(p1_late)
    p2_first()
    p2_down(1)
    p2_up(0)
    p2_down(2)
    p2_up(1)
    p2_up(2)
    g_bases()
    arrived(gains.at[0:3], gain_r.at[0])
    arrived(lims.at[0:3], lim_r.at[0])
    for s in range(3):
        spread(0, s)
    local_done(acts.at[0], loc_sem.at[0])
    first_ready()
    first(0)
    first(1)
    g_cross(0, 3)
    p3_down(1)
    p2_down(3)
    p3_down(2)
    base_ready(TB, 0, t_ready)
    order(TB, 0)
    up_ready(0)
    down_ready(1)
    forward(0, 0)
    p3_up(1)
    p2_up(3)
    forward(0, 1)
    g_cross(3, 6)
    p3_down(3)
    p3_up(2)
    base_ready(TB, 1, t_ready)
    order(TB, 1)
    up_ready(1)
    down_ready(2)
    forward(1, 0)
    p3_up(3)
    forward(1, 1)
    g_cross(6, CHUNKS)
    base_ready(TB, 2, t_ready)
    order(TB, 2)
    spread(1, 3)
    spread(1, 2)
    up_ready(2)
    down_ready(3)
    forward(2, 0)
    forward(2, 1)
    up_ready(3)
    local_done(ups.at[3], loc_sem.at[1])
    back_first(0)
    back_first(1)
    spread(1, 1)
    activate(3, 0)
    activate(3, 1)
    make_grad_up(3)
    send_grad_up(3)
    base_ready(GB, 2, g_ready)
    order(GB, 2)
    backward(3, 0)
    backward(3, 1)
    make_grad_down(3)
    send_grad_down(3)
    make_grad_up(2)
    send_grad_up(2)
    base_ready(GB, 1, g_ready)
    order(GB, 1)
    backward(2, 0)
    relay_up(3)
    backward(2, 1)
    make_grad_down(2)
    make_grad_up(1)
    relay_down(3)
    send_grad_down(2)
    relay_up(2)
    send_grad_up(1)
    base_ready(GB, 0, g_ready)
    order(GB, 0)
    backward(1, 0)
    r2_up(3)
    backward(1, 1)
    make_grad_down(1)
    make_grad_up(0)
    relay_down(2)
    send_grad_down(1)
    relay_up(1)
    send_grad_up(0)
    r2_down(3)
    r2_up(2)
    back_inner(0, 0)
    back_inner(0, 1)
    grad_down_last()
    relay_down(1)
    relay_up(0)
    r2_down(2)
    r2_up(1)
    r3(3, UP)
    r3(3, DOWN)
    r2_last()
    r2_up(0)
    r2_down(1)
    r3(2, UP)
    r3(2, DOWN)
    r3(1, UP)
    r3(0, DOWN)
    r3(0, UP)
    r3(1, DOWN)
    drain()

    scale = 1.0 / math.sqrt(2 * 2048)
    for mat in (UP, DOWN):
        arrived(R3.at[:, mat], r3_r.at[mat])
        total = (R3[0, mat].astype(F32) + R3[1, mat].astype(F32)) * scale
        out_ref[mat] = jnp.transpose(total)

    keeps_r3 = src & (xl == xh)
    pl.when(keeps_r3)(lambda: sent(W.at[0, 0, 0:3], left.at[L_R3]))
    pl.when(src & (xl != xh))(lambda: sent(W.at[0, 0], left.at[L_R3]))


def split(both_ref, down_ref, up_ref):
    down_ref[0] = both_ref[DOWN]
    up_ref[0] = both_ref[UP]


def body(
    inputs,
    cotangent,
    down_weight,
    up_weight,
    section_gains,
    act_bases,
    grad_bases,
    slot_ids,
    act_exps,
    grad_exps,
):
    any_spec = pl.BlockSpec(memory_space=pl.ANY)
    vmem = pl.BlockSpec(memory_space=pltpu.VMEM)
    dma = pltpu.SemaphoreType.DMA
    both = pl.pallas_call(
        kernel,
        out_shape=jax.ShapeDtypeStruct((2, CH, RANK), F32),
        in_specs=[any_spec] * 9 + [pl.BlockSpec(memory_space=pltpu.SMEM)],
        out_specs=vmem,
        scratch_shapes=[
            pltpu.VMEM((4, 2, 4, 2, CH, RANK), BF16),
            pltpu.VMEM((4, CHUNKS, ROWS, CH), BF16),
            pltpu.VMEM((4, CHUNKS, ROWS, CH), BF16),
            pltpu.VMEM((3, CHUNKS, ROWS, CH), BF16),
            pltpu.VMEM((3, CHUNKS, ROWS, CH), BF16),
            pltpu.VMEM((1, WIDTH), BF16),
            pltpu.VMEM((2, ROWS, 64), jnp.int32),
            pltpu.VMEM((4, 1, WIDTH), F32),
            pltpu.VMEM((4, ROWS, 128), BF16),
            pltpu.VMEM((2, CHUNKS, 128, CH), BF16),
            pltpu.VMEM((8, 2, 2, TOK, 128), BF16),
            pltpu.VMEM((8, 2, 3, 2, TOK, 128), BF16),
            pltpu.VMEM((4, ROWS, RANK), F32),
            pltpu.VMEM((4, ROWS, RANK), F32),
            pltpu.VMEM((4, ROWS, RANK), BF16),
            pltpu.VMEM((4, ROWS, RANK), BF16),
            pltpu.VMEM((4, 2, 4, 2, RANK, CH), BF16),
            pltpu.VMEM((4, 3, 4, RANK, CH), BF16),
            pltpu.VMEM((4, 2, 2, RANK, CH), BF16),
            pltpu.VMEM((4, 4, RANK, CH), BF16),
            pltpu.VMEM((4, 2, RANK, CH), BF16),
            pltpu.VMEM((4, 2, 3, RANK, CH), BF16),
            pltpu.VMEM((4, 2, RANK, CH), BF16),
            pltpu.VMEM((2, 2, RANK, CH), BF16),
            pltpu.VMEM((3, 2, RANK // 2, CH), BF16),
            pltpu.VMEM((2, RANK // 2, CH), BF16),
            pltpu.VMEM((4, 2, 2, RANK, CH), BF16),
            pltpu.VMEM((4, 2, RANK, CH), BF16),
            pltpu.VMEM((2, 3, CHUNKS, ROWS, CH), BF16),
            pltpu.VMEM((TOK, CHUNKS * CH), F32),
            pltpu.VMEM((TOK, CHUNKS * CH), BF16),
            dma((4,)),
            dma((3,)),
            dma((3,)),
            dma((1,)),
            dma((1,)),
            dma((4, 2)),
            dma((4, 2)),
            dma((1,)),
            dma((1,)),
            dma((4, 2)),
            dma((4,)),
            dma((4, 2)),
            dma((4, 2)),
            dma((1,)),
            dma((4, 2)),
            dma((2,)),
            dma((8, 2)),
            dma((LEFT_KINDS,)),
        ],
        compiler_params=pltpu.CompilerParams(
            collective_id=0, has_side_effects=True, vmem_limit_bytes=56 * 2**20
        ),
    )(
        inputs.reshape(ROWS, WIDTH),
        cotangent.reshape(ROWS, WIDTH),
        down_weight[0],
        up_weight[0],
        act_bases.reshape(2, ROWS, WIDTH),
        grad_bases.reshape(2, ROWS, WIDTH),
        section_gains,
        act_exps.reshape(ROWS, 64),
        grad_exps.reshape(ROWS, 64),
        slot_ids,
    )
    grad_down, grad_up = pl.pallas_call(
        split,
        out_shape=(jax.ShapeDtypeStruct((1, CH, RANK), F32),) * 2,
        in_specs=[vmem],
        out_specs=(vmem, vmem),
    )(both)
    return grad_down, grad_up


def solution(mesh):
    return jax.shard_map(
        body,
        mesh=mesh,
        in_specs=(
            P(None, "dp", None),
            P(None, "dp", None),
            P("section", "dp", None),
            P("section", "dp", None),
            P("section", None),
            P("section", None, None, "dp", None),
            P("section", None, None, "dp", None),
            P("dp", None),
            P("section", None, "dp", None),
            P("section", None, "dp", None),
        ),
        out_specs=(P("section", "dp", None), P("section", "dp", None)),
        check_vma=False,
    )
```

```python
import functools
import math

import jax
import jax.numpy as jnp
from jax import lax
from jax.experimental import pallas as pl
from jax.experimental.pallas import tpu as pltpu
from jax.sharding import PartitionSpec as P

MESH = pl.DeviceIdType.MESH
F32 = jnp.float32
BF16 = jnp.bfloat16

SECTIONS = 4
WIDTH = 8192
RANK = 128
TOK = 64
ROWS = 2 * TOK
OWN = 256
BL = 128
BLOCKS = 16
CH = 2 * BL
CHUNKS = 8
NORM_EPS = 1e-05
OFF = (1, 3, 2)
DOWN, UP = 0, 1
(
    L_P0,
    L_GAIN,
    L_LIM,
    L_BASE,
    L_W1,
    L_W0,
    L_WD,
    L_WU,
    L_RU,
    L_RD,
    L_RA,
    L_R2,
    L_R3,
    L_X,
    L_XB,
    LEFT_KINDS,
) = range(16)


def dot(a, b):
    return jnp.dot(a, b, preferred_element_type=F32)


def dot_t(a, b):
    return lax.dot_general(a, b, (((1,), (1,)), ((), ())), preferred_element_type=F32)


def kernel(
    x_hbm,
    ct_hbm,
    dw_hbm,
    uw_hbm,
    ab_hbm,
    gb_hbm,
    gain_hbm,
    ae_hbm,
    ge_hbm,
    slot_ref,
    out_ref,
    W,
    acts,
    ups,
    TB,
    GB,
    gain_in,
    gain_out,
    exps_in,
    gains,
    lims,
    sel,
    xs,
    xr,
    inner_all,
    inv_all,
    hid_all,
    bis_all,
    G,
    Q,
    R1,
    S1,
    R1a,
    S1a,
    R1h,
    S1h,
    R2,
    S2,
    R3,
    LX,
    wide,
    narrow,
    loc_sem,
    t_ready,
    g_ready,
    gain_r,
    lim_r,
    p0_r,
    p1_r,
    h1_r,
    h2_r,
    p2_r,
    q_r,
    r1_r,
    a1_r,
    g1_r,
    r2_r,
    r3_r,
    x_r,
    left,
):
    S, J = lax.axis_index("section"), lax.axis_index("dp")
    xh, c = S // 2, S % 2
    y, xl, z = J // 8, (J // 4) % 2, J % 4

    def dp(yy, xx, zz):
        return yy * 8 + xx * 4 + zz

    def at_y(o):
        return (S, dp((y + o) % 4, xl, z))

    def at_z(o):
        return (S, dp(y, xl, (z + o) % 4))

    def group(e):
        return ((S + e) % 4, J)

    def p0_dev(xx, h):
        return (xl * 2 + h, dp(y, xx, z))

    def p0_self(xx, h):
        return (xl * 2 + h == S) & (xl == xx)

    def owner(s):
        return (s, dp(y, xh, z))

    def owner_self(s):
        return (S == s) & (xl == xh)

    def feat(k, h, cc):
        return (k // 4) * 2048 + h * 1024 + (k % 4) * OWN + cc * BL

    def remote(a, b, ss, rs, dev):
        return pltpu.make_async_remote_copy(
            src_ref=a, dst_ref=b, send_sem=ss, recv_sem=rs, device_id=dev, device_id_type=MESH
        )

    def arrived(ref, rs):
        remote(ref, ref, rs, rs, (S, J)).wait_recv()

    def sent(ref, ss):
        remote(ref, ref, ss, ss, (S, J)).wait_send()

    def local_done(ref, sem):
        pltpu.make_async_copy(ref, ref, sem).wait()

    barrier = pltpu.get_barrier_semaphore()

    def greet(dev):
        pl.semaphore_signal(barrier, inc=1, device_id=dev, device_id_type=MESH)

    def greet_all():
        for e in (1, 2, 3):
            greet(group(e))
            greet(at_y(e))
            greet(at_z(e))
        for xx in (0, 1):
            for h in (0, 1):
                @pl.when(jnp.logical_not(p0_self(xx, h)))
                def _():
                    greet(p0_dev(xx, h))
        for s in range(SECTIONS):
            @pl.when(jnp.logical_not(owner_self(s)))
            def _():
                greet(owner(s))

    def place(ref_of, dst, k, h, cc):
        return (
            ref_of.at[:, pl.ds(pl.multiple_of(feat(k, h, cc), BL), BL)],
            dst.at[k // 2, :, pl.ds(pl.multiple_of((k % 2) * BL, BL), BL)],
        )

    def load(ref_of, dst, sem, h, cc):
        def step(k, _):
            pltpu.make_async_copy(*place(ref_of, dst, k, h, cc), sem).start()
            return 0

        lax.fori_loop(0, BLOCKS, step, 0)

    def push(ref_of, dst, ss, rs, h, cc, dev, lo, hi):
        def step(k, _):
            remote(*place(ref_of, dst, k, h, cc), ss, rs, dev).start()
            return 0

        lax.fori_loop(lo, hi, step, 0)

    near = 2 * xh
    holds_mid = c != xh
    lacks_mid = c == xh
    cross = (S + 2) % 4
    sib = xh * 2 + (1 - c)

    greet_all()
    pltpu.make_async_copy(gain_hbm, gain_in, loc_sem.at[2]).start()
    pltpu.make_async_copy(ae_hbm, exps_in.at[0], loc_sem.at[3]).start()
    pltpu.make_async_copy(ge_hbm, exps_in.at[1], loc_sem.at[3]).start()
    load(x_hbm, acts.at[0], loc_sem.at[0], xh, c)
    pl.semaphore_wait(barrier, 9 + 8 - 2 * jnp.where(xl == xh, 1, 0))

    def p0_send():
        for mat, ref in ((DOWN, dw_hbm), (UP, uw_hbm)):
            for xx in (0, 1):
                for h in (0, 1):
                    here, there = ref.at[pl.ds(h * BL, BL)], W.at[S, mat, y, z]

                    @pl.when(jnp.logical_not(p0_self(xx, h)))
                    def _():
                        remote(here, there, left.at[L_P0], p0_r.at[S, mat], p0_dev(xx, h)).start()

                    @pl.when(p0_self(xx, h))
                    def _():
                        pltpu.make_async_copy(here, there, p0_r.at[S, mat]).start()

    pl.when(c == 0)(p0_send)

    pltpu.make_async_copy(gain_hbm, gain_in, loc_sem.at[2]).wait()
    for dst in range(SECTIONS):
        for kk in range(CHUNKS):
            for j in (0, 1):
                row = gain_in[:, pl.ds(feat(2 * kk + j, dst // 2, dst % 2), BL)].astype(F32)
                gain_out[dst, pl.ds(kk, 1), pl.ds(j * BL, BL)] = row
    gains[S] = gain_out[S]
    local_done(exps_in, loc_sem.at[3])
    exps = jnp.concatenate([exps_in[0], exps_in[1]], axis=1)
    limit = jnp.full((ROWS, 128), 448.0 * 2.0**-6, F32)
    for e in (7, 8, 9):
        limit = jnp.where(exps == e, 448.0 * 2.0**-e, limit)
    lims[S] = limit.astype(BF16)
    pl.when(c == 1)(p0_send)
    for e in (1, 2, 3):
        remote(gain_out.at[(S + e) % 4], gains.at[S], left.at[L_GAIN], gain_r.at[0], group(e)).start()
        remote(lims.at[S], lims.at[S], left.at[L_LIM], lim_r.at[0], group(e)).start()

    def build_sel(kk, _):
        b0 = (kk // 2) * 16 + xh * 8 + (kk % 2) * 4 + c
        row = lax.broadcasted_iota(jnp.int32, (128, CH), 0)
        blk = (lax.broadcasted_iota(jnp.int32, (128, CH), 1) // BL) * 2 + b0
        sel[0, kk] = jnp.where(row == blk, 1.0, 0.0).astype(BF16)
        sel[1, kk] = jnp.where(row == blk + 64, 1.0, 0.0).astype(BF16)
        return 0

    def t_bases():
        push(ab_hbm.at[1 - c], TB.at[near], left.at[L_BASE], t_ready.at[near], 1 - xh, c, (cross, J), 0, BLOCKS)
        load(ab_hbm.at[1 - c], TB.at[near], t_ready.at[near], xh, c)

        @pl.when(holds_mid)
        def _():
            push(ab_hbm.at[c], TB.at[1], left.at[L_BASE], t_ready.at[1], xh, 1 - c, (sib, J), 0, BLOCKS)
            load(ab_hbm.at[c], TB.at[1], t_ready.at[1], xh, c)

    def g_bases():
        load(ct_hbm, ups.at[3], loc_sem.at[1], xh, c)
        load(gb_hbm.at[1 - c], GB.at[near], g_ready.at[near], xh, c)

        @pl.when(holds_mid)
        def _():
            push(gb_hbm.at[c], GB.at[1], left.at[L_BASE], g_ready.at[1], xh, 1 - c, (sib, J), 0, BLOCKS)
            load(gb_hbm.at[c], GB.at[1], g_ready.at[1], xh, c)

    def g_cross(lo, hi):
        push(gb_hbm.at[1 - c], GB.at[near], left.at[L_BASE], g_ready.at[near], 1 - xh, c, (cross, J), lo, hi)

    def p0_left():
        pl.when(xl == xh)(lambda: sent(W.at[0, 0, 0:2, 0:3], left.at[L_P0]))
        pl.when(xl != xh)(lambda: sent(W.at[0, 0, 0:2], left.at[L_P0]))

    half = BL // 2
    low, high = pl.ds(0, half), pl.ds(half, half)
    SIDES = ((0, 1), (1, 3))

    def p1_send(s, mat):
        w = W.at[s, mat, y, z]
        arrived(w, p0_r.at[s, mat])
        for o in OFF:
            there = at_y(o) if mat == DOWN else at_z(o)
            remote(w, w, left.at[L_W1], p1_r.at[s, mat], there).start()

    def p1_first(s, mat, i):
        w = W.at[s, mat, y, z]
        arrived(w, p0_r.at[s, mat])
        for o in OFF:
            v = w.at[low]
            remote(v, v, left.at[L_W1], p1_r.at[s, mat], at_y(o)).start()
            v = w.at[high]
            remote(v, v, left.at[L_W1], h1_r.at[i], at_z(o)).start()

    def p2_first(s, mat, i):
        arrived(W.at[s, mat, 0:3, 0, low], p1_r.at[s, mat])
        for o in OFF:
            w = W.at[s, mat, :, z, low]
            remote(w, w, left.at[L_W0], p2_r.at[s, mat], at_z(o)).start()
        arrived(W.at[s, mat, 0, 0:3, high], h1_r.at[i])
        for o in OFF:
            w = W.at[s, mat, y, :, high]
            remote(w, w, left.at[L_W0], h2_r.at[i], at_y(o)).start()

    def first_ready(s, mat, i):
        arrived(W.at[s, mat, :, 0:3, low], p2_r.at[s, mat])
        arrived(W.at[s, mat, 0:3, :, high], h2_r.at[i])

    def p2_down(s):
        arrived(W.at[s, DOWN, 0:3, 0], p1_r.at[s, DOWN])
        for o in OFF:
            w = W.at[s, DOWN, :, z]
            remote(w, w, left.at[L_WD], p2_r.at[s, DOWN], at_z(o)).start()

    def down_ready(s):
        arrived(W.at[s, DOWN, :, 0:3], p2_r.at[s, DOWN])

    def p2_up(s):
        arrived(W.at[s, UP, 0, 0:3], p1_r.at[s, UP])
        for o in OFF:
            w = W.at[s, UP, y]
            remote(w, w, left.at[L_WU], p2_r.at[s, UP], at_y(o)).start()

    def up_ready(s):
        arrived(W.at[s, UP, 0:3], p2_r.at[s, UP])

    def pair(d):
        return pl.ds(2 * d, 2)

    def rows(m):
        return pl.ds(m * TOK, TOK)

    def gain_row(s, kk):
        return gains[s, pl.ds(kk, 1), :]

    def rows_of(s, mat, kk):
        return W[s, mat, kk // 2, pl.ds((kk % 2) * 2, 2)].reshape(CH, RANK)

    def fold(v):
        return v[:, :128] + v[:, 128:]

    def chunk_loop(step, init):
        return lax.fori_loop(0, CHUNKS, step, init, unroll=True)

    def x_send(ex, m):
        for e in (1, 2, 3):
            remote(
                xs.at[ex, m], xr.at[ex, m, e - 1], left.at[L_X], x_r.at[ex, m], group(e)
            ).start()

    inner_rows, square_rows = pl.ds(0, TOK), pl.ds(TOK, 16)

    def x_total(ex, m, part):
        total = xs[ex, m, part, :].astype(F32)
        for e in range(3):
            total = total + xr[ex, m, e, part, :].astype(F32)
        return total

    def diagonal(v):
        shape = (TOK, 128)
        here = lax.broadcasted_iota(jnp.int32, shape, 0) == lax.broadcasted_iota(jnp.int32, shape, 1)
        return jnp.where(here, v, 0.0)

    def x_wait(ex, m):
        arrived(xr.at[ex, m], x_r.at[ex, m])

    zero = jnp.zeros((TOK, 128), F32)

    def enter(s, kk, value, inner, sq):
        full = value.astype(F32)
        sq = sq + fold(full * full)
        scaled = (full * gain_row(s, kk)).astype(BF16)
        return inner + dot(scaled, rows_of(s, DOWN, kk)), sq

    def hand_over(ex, m, inner, sq):
        row = jnp.sum(diagonal(jnp.sum(sq, axis=-1, keepdims=True)), axis=0, keepdims=True)
        coarse = row.astype(BF16).astype(F32)
        upper = lax.broadcasted_iota(jnp.int32, (16, 128), 0) < 8
        xs[ex, m, inner_rows, :] = inner.astype(BF16)
        xs[ex, m, square_rows, :] = jnp.where(upper, coarse, row - coarse).astype(BF16)
        x_send(ex, m)

    def first(m):
        def step(kk, carry):
            return enter(0, kk, acts[0, kk, rows(m), :], *carry)

        inner, sq = chunk_loop(step, (zero, zero))
        hand_over(0, m, inner, sq)

    def activate(s, m):
        x_wait(s, m)
        squares = x_total(s, m, square_rows)
        row = squares[0:1, :] + squares[8:9, :]
        mean = jnp.sum(diagonal(row), axis=-1, keepdims=True) * (1.0 / WIDTH)
        inv = jnp.broadcast_to(lax.rsqrt(mean + NORM_EPS), (TOK, 128))
        inner = x_total(s, m, inner_rows) * inv
        hid = (inner * jax.nn.sigmoid(inner)).astype(BF16)
        inner_all[s, rows(m), :] = inner
        inv_all[s, rows(m), :] = inv
        hid_all[s, rows(m), :] = hid
        return hid

    def spread(t, s):
        def step(kk, _):
            LX[t, s - t, kk] = dot(lims[s], sel[t, kk]).astype(BF16)
            return 0

        chunk_loop(step, 0)

    def order(table, b):
        straight = jnp.full((TOK, CH), slot_ref[0, 0]) == 0

        def step(kk, _):
            one = table[b, kk, 0:TOK, :].astype(F32)
            two = table[b, kk, TOK:ROWS, :].astype(F32)
            table[b, kk, 0:TOK, :] = jnp.where(straight, one, two).astype(BF16)
            table[b, kk, TOK:ROWS, :] = jnp.where(straight, two, one).astype(BF16)
            return 0

        chunk_loop(step, 0)

    def recode(value, base, limit):
        base, limit = base.astype(F32), limit.astype(F32)
        delta = jnp.minimum(jnp.maximum(value - base, -limit), limit).astype(BF16)
        return (base + delta.astype(F32)).astype(BF16)

    def cols(kk):
        return pl.ds(pl.multiple_of(kk * CH, CH), CH)

    def flat(s, mat):
        return W[s, mat].reshape(CHUNKS * CH, RANK)

    def forward(s, m):
        hid = activate(s, m)
        wide[...] = dot_t(hid, flat(s, UP))

        def step(kk, sq):
            out = acts[s, kk, rows(m), :].astype(F32) + wide[:, cols(kk)]
            value = recode(out, TB[s, kk, rows(m), :], LX[0, s, kk, rows(m), :])
            acts[s + 1, kk, rows(m), :] = value
            full = value.astype(F32)
            narrow[:, cols(kk)] = (full * gain_row(s + 1, kk)).astype(BF16)
            return sq + fold(full * full)

        sq = chunk_loop(step, zero)
        hand_over(s + 1, m, dot(narrow[...], flat(s + 1, DOWN)), sq)

    def back_first(m):
        def step(kk, carry):
            return carry + dot(ups[3, kk, rows(m), :], rows_of(3, UP, kk))

        xs[4 + 3, m, inner_rows, :] = chunk_loop(step, zero).astype(BF16)
        xb_send(3, m)

    def xb_send(s, m):
        for e in (1, 2, 3):
            remote(
                xs.at[4 + s, m, inner_rows],
                xr.at[4 + s, m, e - 1, inner_rows],
                left.at[L_XB],
                x_r.at[4 + s, m],
                group(e),
            ).start()

    def back_inner(s, m):
        arrived(xr.at[4 + s, m, :, inner_rows], x_r.at[4 + s, m])
        inner, inv = inner_all[s, rows(m), :], inv_all[s, rows(m), :]
        sig = jax.nn.sigmoid(inner)
        bi = x_total(4 + s, m, inner_rows) * sig * (1.0 + inner * (1.0 - sig)) * inv
        bis = bi.astype(BF16)
        bis_all[s, rows(m), :] = bis
        coef = jnp.sum(bis.astype(F32) * inner * inv, axis=-1, keepdims=True) * (1.0 / WIDTH)
        return bis, jnp.broadcast_to(coef, (TOK, CH))

    def backward(s, m):
        bis, coef = back_inner(s, m)
        wide[...] = dot_t(bis, flat(s, DOWN))

        def step(kk, _):
            value = (
                ups[s, kk, rows(m), :].astype(F32)
                + wide[:, cols(kk)] * gain_row(s, kk)
                - acts[s, kk, rows(m), :].astype(F32) * coef
            )
            value = recode(value, GB[s - 1, kk, rows(m), :], LX[1, s - 1, kk, rows(m), :])
            ups[s - 1, kk, rows(m), :] = value
            narrow[:, cols(kk)] = value
            return 0

        chunk_loop(step, 0)
        xs[4 + s - 1, m, inner_rows, :] = dot(narrow[...], flat(s - 1, UP)).astype(BF16)
        xb_send(s - 1, m)

    def keep(s, mat, kk, value):
        value = value.astype(BF16)
        G[s, mat, kk // 2, (kk % 2) * 2] = value[:, :BL]
        G[s, mat, kk // 2, (kk % 2) * 2 + 1] = value[:, BL:]

    def make_grad_up(s):
        turned = jnp.transpose(hid_all[s].astype(F32)).astype(BF16)

        def step(kk, _):
            keep(s, UP, kk, dot(turned, ups[s, kk]))
            return 0

        chunk_loop(step, 0)

    def make_grad_down(s):
        turned = jnp.transpose(bis_all[s].astype(F32)).astype(BF16)

        def step(kk, _):
            keep(s, DOWN, kk, dot(turned, acts[s, kk]) * gain_row(s, kk))
            return 0

        chunk_loop(step, 0)

    rlow, rhigh = pl.ds(0, RANK // 2), pl.ds(RANK // 2, RANK // 2)

    def part(s, mat, o, which):
        if mat == UP:
            return G.at[s, UP, (y + o) % 4, which]
        return G.at[s, DOWN, which, (z + o) % 4]

    def ring(mat):
        return at_y if mat == UP else at_z

    def kind(mat):
        return left.at[L_RU] if mat == UP else left.at[L_RD]

    def grad_down_last():
        make_grad_down(0)
        for d, o in enumerate(OFF):
            remote(
                G.at[0, DOWN, :, (z + o) % 4, rlow], R1a.at[d], left.at[L_RA], a1_r.at[0], at_z(o)
            ).start()
            remote(
                G.at[0, DOWN, (y + o) % 4, :, rhigh], R1h.at[d], left.at[L_RA], g1_r.at[0], at_y(o)
            ).start()

    def send_grad(s, mat):
        for d, o in SIDES:
            remote(part(s, mat, 2, pair(d)), Q.at[s, mat, d], kind(mat), q_r.at[s, mat], ring(mat)(o)).start()
        for d, o in SIDES:
            remote(
                part(s, mat, o, pair(1 - d)),
                R1.at[s, mat, d, pair(1 - d)],
                kind(mat),
                r1_r.at[s, mat],
                ring(mat)(o),
            ).start()

    def relay(s, mat):
        arrived(Q.at[s, mat], q_r.at[s, mat])
        for d, o in SIDES:
            for j in range(2):
                ref = part(s, mat, o, 2 * d + j)
                ref[...] = (ref[...].astype(F32) + Q[s, mat, d, j].astype(F32)).astype(BF16)
            remote(
                part(s, mat, o, pair(d)), R1.at[s, mat, d, pair(d)], kind(mat), r1_r.at[s, mat], ring(mat)(o)
            ).start()

    def add_up(a, parts):
        total = a.astype(F32)
        for value in parts:
            total = total + value.astype(F32)
        return total.astype(BF16)

    def r2(s, mat):
        arrived(R1.at[s, mat], r1_r.at[s, mat])
        for j in range(4):
            S1[s, mat, j] = add_up(part(s, mat, 0, j)[...], [R1[s, mat, d, j] for d in range(2)])
        for d, o in enumerate(OFF):
            there, j = (at_z(o), (z + o) % 4) if mat == UP else (at_y(o), (y + o) % 4)
            remote(S1.at[s, mat, j], R2.at[s, mat, d], left.at[L_R2], r2_r.at[s, mat], there).start()

    def r2_last():
        arrived(R1a, a1_r.at[0])
        for j in range(4):
            S1a[j] = add_up(G[0, DOWN, j, z, rlow, :], [R1a[d, j] for d in range(3)])
        for d, o in enumerate(OFF):
            remote(
                S1a.at[(y + o) % 4], R2.at[0, DOWN, d, rlow], left.at[L_R2], r2_r.at[0, DOWN], at_y(o)
            ).start()
        arrived(R1h, g1_r.at[0])
        for j in range(4):
            S1h[j] = add_up(G[0, DOWN, y, j, rhigh, :], [R1h[d, j] for d in range(3)])
        for d, o in enumerate(OFF):
            remote(
                S1h.at[(z + o) % 4], R2.at[0, DOWN, d, rhigh], left.at[L_R2], r2_r.at[0, DOWN], at_z(o)
            ).start()

    def r3(s, mat):
        arrived(R2.at[s, mat], r2_r.at[s, mat])
        if s == 0 and mat == DOWN:
            for some, own in ((rlow, S1a[y]), (rhigh, S1h[z])):
                S2[s, mat, some, :] = add_up(own, [R2[s, mat, d, some, :] for d in range(3)])
        else:
            own = S1[s, mat, z if mat == UP else y]
            S2[s, mat] = add_up(own, [R2[s, mat, d] for d in range(3)])

        @pl.when(jnp.logical_not(owner_self(s)))
        def _():
            remote(S2.at[s, mat], R3.at[xl, c, mat], left.at[L_R3], r3_r.at[mat], owner(s)).start()

        @pl.when(owner_self(s))
        def _():
            pltpu.make_async_copy(S2.at[s, mat], R3.at[xl, c, mat], r3_r.at[mat]).start()

    def base_ready(table, b, sems):
        arrived(table.at[b], sems.at[b])

    def drain():
        p0_left()
        sent(gains.at[0:3], left.at[L_GAIN])
        sent(lims.at[0:3], left.at[L_LIM])
        pl.when(holds_mid)(lambda: sent(acts, left.at[L_BASE]))
        pl.when(lacks_mid)(lambda: sent(TB.at[0:2], left.at[L_BASE]))
        sent(W.at[0:3, 0, 0:2], left.at[L_W1])
        sent(W.at[0:3, 0, 0:2], left.at[L_W0])
        sent(W.at[0:3, 0, 0:3], left.at[L_WD])
        sent(W.at[0:3, 0, 0:3], left.at[L_WU])
        sent(W.at[0:3, 0], left.at[L_RU])
        sent(W.at[0:3, 0, 0:3], left.at[L_RD])
        sent(W.at[0, 0, 0:3], left.at[L_RA])
        sent(W.at[0:3, 0, 0:2], left.at[L_R2])
        sent(xr.at[0:4], left.at[L_X])
        sent(xr.at[4:8, :, :, inner_rows], left.at[L_XB])

    lax.fori_loop(0, CHUNKS, build_sel, 0)

    def p1_late():
        p1_send(2, DOWN)
        p1_send(3, DOWN)
        p1_send(2, UP)
        p1_first(3, UP, 1)

    t_bases()
    holds_late = (xh == 1) & (xl == 1)
    pl.when(holds_late)(p1_late)
    p1_first(0, DOWN, 0)
    p1_send(1, DOWN)
    p1_send(0, UP)
    p1_send(1, UP)
    pl.when(jnp.logical_not(holds_late))(p1_late)
    p2_first(0, DOWN, 0)
    p2_up(0)
    p2_down(1)
    g_bases()
    arrived(gains.at[0:3], gain_r.at[0])
    arrived(lims.at[0:3], lim_r.at[0])
    for s in range(3):
        spread(0, s)
    p2_up(1)
    local_done(acts.at[0], loc_sem.at[0])
    first_ready(0, DOWN, 0)
    first(0)
    first(1)
    p2_down(2)
    p2_up(2)
    p2_down(3)
    p2_first(3, UP, 1)
    g_cross(0, 6)
    for s in range(3):
        base_ready(TB, s, t_ready)
        order(TB, s)
        if s == 2:
            spread(1, 3)
            spread(1, 2)
        up_ready(s)
        down_ready(s + 1)
        forward(s, 0)
        forward(s, 1)
        if s < 2:
            g_cross(6 * s + 6, min(6 * s + 12, BLOCKS))
    first_ready(3, UP, 1)
    local_done(ups.at[3], loc_sem.at[1])
    back_first(0)
    back_first(1)
    spread(1, 1)
    activate(3, 0)
    activate(3, 1)
    make_grad_up(3)
    send_grad(3, UP)
    base_ready(GB, 2, g_ready)
    order(GB, 2)
    backward(3, 0)
    backward(3, 1)
    make_grad_down(3)
    send_grad(3, DOWN)
    make_grad_up(2)
    send_grad(2, UP)
    base_ready(GB, 1, g_ready)
    order(GB, 1)
    relay(3, UP)
    backward(2, 0)
    backward(2, 1)
    make_grad_down(2)
    make_grad_up(1)
    relay(3, DOWN)
    send_grad(2, DOWN)
    relay(2, UP)
    send_grad(1, UP)
    base_ready(GB, 0, g_ready)
    order(GB, 0)
    r2(3, UP)
    backward(1, 0)
    backward(1, 1)
    make_grad_down(1)
    make_grad_up(0)
    r2(3, DOWN)
    relay(2, DOWN)
    send_grad(1, DOWN)
    send_grad(0, UP)
    relay(1, UP)
    back_inner(0, 0)
    back_inner(0, 1)
    grad_down_last()
    r2(2, UP)
    relay(0, UP)
    relay(1, DOWN)
    r2(2, DOWN)
    r2(1, UP)
    r2_last()
    r2(0, UP)
    r2(1, DOWN)
    r3(3, UP)
    r3(3, DOWN)
    r3(2, UP)
    r3(2, DOWN)
    r3(1, UP)
    r3(0, DOWN)
    r3(0, UP)
    r3(1, DOWN)
    drain()

    scale = 1.0 / math.sqrt(2 * 2048)
    for mat in (UP, DOWN):
        arrived(R3.at[:, :, mat], r3_r.at[mat])
        for h in (0, 1):
            total = (R3[0, h, mat].astype(F32) + R3[1, h, mat].astype(F32)) * scale
            out_ref[mat, pl.ds(h * BL, BL), :] = jnp.transpose(total)

    pl.when(xl == xh)(lambda: sent(W.at[0, 0, 0:2, 0:3], left.at[L_R3]))
    pl.when(xl != xh)(lambda: sent(W.at[0, 0, 0:2], left.at[L_R3]))


def split(both_ref, down_ref, up_ref):
    down_ref[0] = both_ref[DOWN]
    up_ref[0] = both_ref[UP]


def body(
    inputs,
    cotangent,
    down_weight,
    up_weight,
    section_gains,
    act_bases,
    grad_bases,
    slot_ids,
    act_exps,
    grad_exps,
):
    any_spec = pl.BlockSpec(memory_space=pl.ANY)
    vmem = pl.BlockSpec(memory_space=pltpu.VMEM)
    dma = pltpu.SemaphoreType.DMA
    both = pl.pallas_call(
        kernel,
        out_shape=jax.ShapeDtypeStruct((2, OWN, RANK), F32),
        in_specs=[any_spec] * 9 + [pl.BlockSpec(memory_space=pltpu.SMEM)],
        out_specs=vmem,
        scratch_shapes=[
            pltpu.VMEM((4, 2, 4, 4, BL, RANK), BF16),
            pltpu.VMEM((4, CHUNKS, ROWS, CH), BF16),
            pltpu.VMEM((4, CHUNKS, ROWS, CH), BF16),
            pltpu.VMEM((3, CHUNKS, ROWS, CH), BF16),
            pltpu.VMEM((3, CHUNKS, ROWS, CH), BF16),
            pltpu.VMEM((1, WIDTH), BF16),
            pltpu.VMEM((4, CHUNKS, CH), F32),
            pltpu.VMEM((2, ROWS, 64), jnp.int32),
            pltpu.VMEM((4, CHUNKS, CH), F32),
            pltpu.VMEM((4, ROWS, 128), BF16),
            pltpu.VMEM((2, CHUNKS, 128, CH), BF16),
            pltpu.VMEM((8, 2, TOK + 16, 128), BF16),
            pltpu.VMEM((8, 2, 3, TOK + 16, 128), BF16),
            pltpu.VMEM((4, ROWS, RANK), F32),
            pltpu.VMEM((4, ROWS, RANK), F32),
            pltpu.VMEM((4, ROWS, RANK), BF16),
            pltpu.VMEM((4, ROWS, RANK), BF16),
            pltpu.VMEM((4, 2, 4, 4, RANK, BL), BF16),
            pltpu.VMEM((4, 2, 2, 2, RANK, BL), BF16),
            pltpu.VMEM((4, 2, 2, 4, RANK, BL), BF16),
            pltpu.VMEM((4, 2, 4, RANK, BL), BF16),
            pltpu.VMEM((3, 4, RANK // 2, BL), BF16),
            pltpu.VMEM((4, RANK // 2, BL), BF16),
            pltpu.VMEM((3, 4, RANK // 2, BL), BF16),
            pltpu.VMEM((4, RANK // 2, BL), BF16),
            pltpu.VMEM((4, 2, 3, RANK, BL), BF16),
            pltpu.VMEM((4, 2, RANK, BL), BF16),
            pltpu.VMEM((2, 2, 2, RANK, BL), BF16),
            pltpu.VMEM((2, 3, CHUNKS, ROWS, CH), BF16),
            pltpu.VMEM((TOK, CHUNKS * CH), F32),
            pltpu.VMEM((TOK, CHUNKS * CH), BF16),
            dma((4,)),
            dma((3,)),
            dma((3,)),
            dma((1,)),
            dma((1,)),
            dma((4, 2)),
            dma((4, 2)),
            dma((2,)),
            dma((2,)),
            dma((4, 2)),
            dma((4, 2)),
            dma((4, 2)),
            dma((1,)),
            dma((1,)),
            dma((4, 2)),
            dma((2,)),
            dma((8, 2)),
            dma((LEFT_KINDS,)),
        ],
        compiler_params=pltpu.CompilerParams(
            collective_id=0, has_side_effects=True, vmem_limit_bytes=56 * 2**20
        ),
    )(
        inputs.reshape(ROWS, WIDTH),
        cotangent.reshape(ROWS, WIDTH),
        down_weight[0],
        up_weight[0],
        act_bases.reshape(2, ROWS, WIDTH),
        grad_bases.reshape(2, ROWS, WIDTH),
        section_gains,
        act_exps.reshape(ROWS, 64),
        grad_exps.reshape(ROWS, 64),
        slot_ids,
    )
    grad_down, grad_up = pl.pallas_call(
        split,
        out_shape=(jax.ShapeDtypeStruct((1, OWN, RANK), F32),) * 2,
        in_specs=[vmem],
        out_specs=(vmem, vmem),
    )(both)
    return grad_down, grad_up


def solution(mesh):
    return jax.shard_map(
        body,
        mesh=mesh,
        in_specs=(
            P(None, "dp", None),
            P(None, "dp", None),
            P("section", "dp", None),
            P("section", "dp", None),
            P("section", None),
            P("section", None, None, "dp", None),
            P("section", None, None, "dp", None),
            P("dp", None),
            P("section", None, "dp", None),
            P("section", None, "dp", None),
        ),
        out_specs=(P("section", "dp", None), P("section", "dp", None)),
        check_vma=False,
    )
```

```python
import functools
import math

import jax
import jax.numpy as jnp
from jax import lax
from jax.experimental import pallas as pl
from jax.experimental.pallas import tpu as pltpu
from jax.sharding import PartitionSpec as P

MESH = pl.DeviceIdType.MESH
F32 = jnp.float32
BF16 = jnp.bfloat16

SECTIONS = 4
WIDTH = 8192
RANK = 128
TOK = 64
ROWS = 2 * TOK
OWN = 256
BL = 128
BLOCKS = 16
CH = 2 * BL
CHUNKS = 8
NORM_EPS = 1e-05
OFF = (1, 3, 2)
DOWN, UP = 0, 1
(
    L_P0,
    L_GAIN,
    L_LIM,
    L_BASE,
    L_W1,
    L_W0,
    L_WD,
    L_WU,
    L_RU,
    L_RD,
    L_RA,
    L_R2,
    L_R3,
    L_X,
    L_XB,
    LEFT_KINDS,
) = range(16)


def dot(a, b):
    return jnp.dot(a, b, preferred_element_type=F32)


def dot_t(a, b):
    return lax.dot_general(a, b, (((1,), (1,)), ((), ())), preferred_element_type=F32)


def kernel(
    x_hbm,
    ct_hbm,
    dw_hbm,
    uw_hbm,
    ab_hbm,
    gb_hbm,
    gain_hbm,
    ae_hbm,
    ge_hbm,
    slot_ref,
    out_hbm,
    W,
    acts,
    ups,
    TB,
    GB,
    gain_in,
    gain_out,
    exps_in,
    gains,
    lims,
    sel,
    xs,
    xr,
    inner_all,
    inv_all,
    hid_all,
    bis_all,
    G,
    Q,
    R1,
    S1,
    R1a,
    S1a,
    R1h,
    S1h,
    R2,
    S2,
    R3,
    LX,
    wide,
    narrow,
    result,
    out_sem,
    loc_sem,
    t_ready,
    g_ready,
    gain_r,
    lim_r,
    p0_r,
    p1_r,
    h1_r,
    h2_r,
    p2_r,
    q_r,
    r1_r,
    a1_r,
    g1_r,
    r2_r,
    r3_r,
    x_r,
    left,
):
    S, J = lax.axis_index("section"), lax.axis_index("dp")
    xh, c = S // 2, S % 2
    y, xl, z = J // 8, (J // 4) % 2, J % 4

    def dp(yy, xx, zz):
        return yy * 8 + xx * 4 + zz

    def at_y(o):
        return (S, dp((y + o) % 4, xl, z))

    def at_z(o):
        return (S, dp(y, xl, (z + o) % 4))

    def group(e):
        return ((S + e) % 4, J)

    def p0_dev(xx, h):
        return (xl * 2 + h, dp(y, xx, z))

    def p0_self(xx, h):
        return (xl * 2 + h == S) & (xl == xx)

    def owner(s):
        return (s, dp(y, xh, z))

    def owner_self(s):
        return (S == s) & (xl == xh)

    def feat(k, h, cc):
        return (k // 4) * 2048 + h * 1024 + (k % 4) * OWN + cc * BL

    def remote(a, b, ss, rs, dev):
        return pltpu.make_async_remote_copy(
            src_ref=a, dst_ref=b, send_sem=ss, recv_sem=rs, device_id=dev, device_id_type=MESH
        )

    def arrived(ref, rs):
        remote(ref, ref, rs, rs, (S, J)).wait_recv()

    def sent(ref, ss):
        remote(ref, ref, ss, ss, (S, J)).wait_send()

    def local_done(ref, sem):
        pltpu.make_async_copy(ref, ref, sem).wait()

    barrier = pltpu.get_barrier_semaphore()

    def greet(dev):
        pl.semaphore_signal(barrier, inc=1, device_id=dev, device_id_type=MESH)

    def greet_all():
        for e in (1, 2, 3):
            greet(group(e))
            greet(at_y(e))
            greet(at_z(e))
        for xx in (0, 1):
            for h in (0, 1):
                @pl.when(jnp.logical_not(p0_self(xx, h)))
                def _():
                    greet(p0_dev(xx, h))
        for s in range(SECTIONS):
            @pl.when(jnp.logical_not(owner_self(s)))
            def _():
                greet(owner(s))

    def place(ref_of, dst, k, h, cc):
        return (
            ref_of.at[:, pl.ds(pl.multiple_of(feat(k, h, cc), BL), BL)],
            dst.at[k // 2, :, pl.ds(pl.multiple_of((k % 2) * BL, BL), BL)],
        )

    def load(ref_of, dst, sem, h, cc):
        def step(k, _):
            pltpu.make_async_copy(*place(ref_of, dst, k, h, cc), sem).start()
            return 0

        lax.fori_loop(0, BLOCKS, step, 0)

    def push(ref_of, dst, ss, rs, h, cc, dev, lo, hi):
        def step(k, _):
            remote(*place(ref_of, dst, k, h, cc), ss, rs, dev).start()
            return 0

        lax.fori_loop(lo, hi, step, 0)

    near = 2 * xh
    holds_mid = c != xh
    lacks_mid = c == xh
    cross = (S + 2) % 4
    sib = xh * 2 + (1 - c)

    greet_all()
    pltpu.make_async_copy(gain_hbm, gain_in, loc_sem.at[2]).start()
    pltpu.make_async_copy(ae_hbm, exps_in.at[0], loc_sem.at[3]).start()
    pltpu.make_async_copy(ge_hbm, exps_in.at[1], loc_sem.at[3]).start()
    load(x_hbm, acts.at[0], loc_sem.at[0], xh, c)
    pl.semaphore_wait(barrier, 9 + 8 - 2 * jnp.where(xl == xh, 1, 0))

    def p0_send(mat):
        ref = dw_hbm if mat == DOWN else uw_hbm
        for xx in (0, 1):
            for h in (0, 1):
                here, there = ref.at[pl.ds(h * BL, BL)], W.at[S, mat, y, z]

                @pl.when(jnp.logical_not(p0_self(xx, h)))
                def _():
                    remote(here, there, left.at[L_P0], p0_r.at[S, mat], p0_dev(xx, h)).start()

                @pl.when(p0_self(xx, h))
                def _():
                    pltpu.make_async_copy(here, there, p0_r.at[S, mat]).start()

    pl.when(c == 0)(lambda: p0_send(DOWN))

    pltpu.make_async_copy(gain_hbm, gain_in, loc_sem.at[2]).wait()
    for dst in range(SECTIONS):
        for kk in range(CHUNKS):
            for j in (0, 1):
                row = gain_in[:, pl.ds(feat(2 * kk + j, dst // 2, dst % 2), BL)].astype(F32)
                gain_out[dst, pl.ds(kk, 1), pl.ds(j * BL, BL)] = row
    gains[S] = gain_out[S]
    local_done(exps_in, loc_sem.at[3])
    exps = jnp.concatenate([exps_in[0], exps_in[1]], axis=1)
    limit = jnp.full((ROWS, 128), 448.0 * 2.0**-6, F32)
    for e in (7, 8, 9):
        limit = jnp.where(exps == e, 448.0 * 2.0**-e, limit)
    lims[S] = limit.astype(BF16)
    pl.when(c == 1)(lambda: p0_send(DOWN))
    p0_send(UP)
    for e in (1, 2, 3):
        remote(gain_out.at[(S + e) % 4], gains.at[S], left.at[L_GAIN], gain_r.at[0], group(e)).start()
        remote(lims.at[S], lims.at[S], left.at[L_LIM], lim_r.at[0], group(e)).start()

    def build_sel(kk, _):
        b0 = (kk // 2) * 16 + xh * 8 + (kk % 2) * 4 + c
        row = lax.broadcasted_iota(jnp.int32, (128, CH), 0)
        blk = (lax.broadcasted_iota(jnp.int32, (128, CH), 1) // BL) * 2 + b0
        sel[0, kk] = jnp.where(row == blk, 1.0, 0.0).astype(BF16)
        sel[1, kk] = jnp.where(row == blk + 64, 1.0, 0.0).astype(BF16)
        return 0

    def t_bases():
        push(ab_hbm.at[1 - c], TB.at[near], left.at[L_BASE], t_ready.at[near], 1 - xh, c, (cross, J), 0, BLOCKS)
        load(ab_hbm.at[1 - c], TB.at[near], t_ready.at[near], xh, c)

        @pl.when(holds_mid)
        def _():
            push(ab_hbm.at[c], TB.at[1], left.at[L_BASE], t_ready.at[1], xh, 1 - c, (sib, J), 0, BLOCKS)
            load(ab_hbm.at[c], TB.at[1], t_ready.at[1], xh, c)

    def g_bases():
        load(ct_hbm, ups.at[3], loc_sem.at[1], xh, c)
        load(gb_hbm.at[1 - c], GB.at[near], g_ready.at[near], xh, c)

        @pl.when(holds_mid)
        def _():
            push(gb_hbm.at[c], GB.at[1], left.at[L_BASE], g_ready.at[1], xh, 1 - c, (sib, J), 0, BLOCKS)
            load(gb_hbm.at[c], GB.at[1], g_ready.at[1], xh, c)

    def g_cross(lo, hi):
        push(gb_hbm.at[1 - c], GB.at[near], left.at[L_BASE], g_ready.at[near], 1 - xh, c, (cross, J), lo, hi)

    def p0_left():
        pl.when(xl == xh)(lambda: sent(W.at[0, 0, 0:2, 0:3], left.at[L_P0]))
        pl.when(xl != xh)(lambda: sent(W.at[0, 0, 0:2], left.at[L_P0]))

    half = BL // 2
    low, high = pl.ds(0, half), pl.ds(half, half)
    SIDES = ((0, 1), (1, 3))

    def p1_send(s, mat):
        w = W.at[s, mat, y, z]
        arrived(w, p0_r.at[s, mat])
        for o in OFF:
            there = at_y(o) if mat == DOWN else at_z(o)
            remote(w, w, left.at[L_W1], p1_r.at[s, mat], there).start()

    def p1_first(s, mat, i):
        w = W.at[s, mat, y, z]
        arrived(w, p0_r.at[s, mat])
        for o in OFF:
            v = w.at[low]
            remote(v, v, left.at[L_W1], p1_r.at[s, mat], at_y(o)).start()
            v = w.at[high]
            remote(v, v, left.at[L_W1], h1_r.at[i], at_z(o)).start()

    def p2_first(s, mat, i):
        arrived(W.at[s, mat, 0:3, 0, low], p1_r.at[s, mat])
        for o in OFF:
            w = W.at[s, mat, :, z, low]
            remote(w, w, left.at[L_W0], p2_r.at[s, mat], at_z(o)).start()
        arrived(W.at[s, mat, 0, 0:3, high], h1_r.at[i])
        for o in OFF:
            w = W.at[s, mat, y, :, high]
            remote(w, w, left.at[L_W0], h2_r.at[i], at_y(o)).start()

    def first_ready(s, mat, i):
        arrived(W.at[s, mat, :, 0:3, low], p2_r.at[s, mat])
        arrived(W.at[s, mat, 0:3, :, high], h2_r.at[i])

    def p2_down(s):
        arrived(W.at[s, DOWN, 0:3, 0], p1_r.at[s, DOWN])
        for o in OFF:
            w = W.at[s, DOWN, :, z]
            remote(w, w, left.at[L_WD], p2_r.at[s, DOWN], at_z(o)).start()

    def down_ready(s):
        arrived(W.at[s, DOWN, :, 0:3], p2_r.at[s, DOWN])

    def p2_up(s):
        arrived(W.at[s, UP, 0, 0:3], p1_r.at[s, UP])
        for o in OFF:
            w = W.at[s, UP, y]
            remote(w, w, left.at[L_WU], p2_r.at[s, UP], at_y(o)).start()

    def up_ready(s):
        arrived(W.at[s, UP, 0:3], p2_r.at[s, UP])

    def pair(d):
        return pl.ds(2 * d, 2)

    def rows(m):
        return pl.ds(m * TOK, TOK)

    def gain_row(s, kk):
        return gains[s, pl.ds(kk, 1), :]

    def rows_of(s, mat, kk):
        return W[s, mat, kk // 2, pl.ds((kk % 2) * 2, 2)].reshape(CH, RANK)

    def fold(v):
        return v[:, :128] + v[:, 128:]

    def chunk_loop(step, init):
        return lax.fori_loop(0, CHUNKS, step, init, unroll=True)

    def x_send(ex, m):
        for e in (1, 2, 3):
            remote(
                xs.at[ex, m], xr.at[ex, m, e - 1], left.at[L_X], x_r.at[ex, m], group(e)
            ).start()

    inner_rows, square_rows = pl.ds(0, TOK), pl.ds(TOK, 16)

    def x_total(ex, m, part):
        total = xs[ex, m, part, :].astype(F32)
        for e in range(3):
            total = total + xr[ex, m, e, part, :].astype(F32)
        return total

    def diagonal(v):
        shape = (TOK, 128)
        here = lax.broadcasted_iota(jnp.int32, shape, 0) == lax.broadcasted_iota(jnp.int32, shape, 1)
        return jnp.where(here, v, 0.0)

    def x_wait(ex, m):
        arrived(xr.at[ex, m], x_r.at[ex, m])

    zero = jnp.zeros((TOK, 128), F32)

    def enter(s, kk, value, inner, sq):
        full = value.astype(F32)
        sq = sq + fold(full * full)
        scaled = (full * gain_row(s, kk)).astype(BF16)
        return inner + dot(scaled, rows_of(s, DOWN, kk)), sq

    def hand_over(ex, m, inner, sq):
        row = jnp.sum(diagonal(jnp.sum(sq, axis=-1, keepdims=True)), axis=0, keepdims=True)
        coarse = row.astype(BF16).astype(F32)
        upper = lax.broadcasted_iota(jnp.int32, (16, 128), 0) < 8
        xs[ex, m, inner_rows, :] = inner.astype(BF16)
        xs[ex, m, square_rows, :] = jnp.where(upper, coarse, row - coarse).astype(BF16)
        x_send(ex, m)

    def first(m):
        def step(kk, carry):
            return enter(0, kk, acts[0, kk, rows(m), :], *carry)

        inner, sq = chunk_loop(step, (zero, zero))
        hand_over(0, m, inner, sq)

    def activate(s, m):
        x_wait(s, m)
        squares = x_total(s, m, square_rows)
        row = squares[0:1, :] + squares[8:9, :]
        mean = jnp.sum(diagonal(row), axis=-1, keepdims=True) * (1.0 / WIDTH)
        inv = jnp.broadcast_to(lax.rsqrt(mean + NORM_EPS), (TOK, 128))
        inner = x_total(s, m, inner_rows) * inv
        hid = (inner * jax.nn.sigmoid(inner)).astype(BF16)
        inner_all[s, rows(m), :] = inner
        inv_all[s, rows(m), :] = inv
        hid_all[s, rows(m), :] = hid
        return hid

    def spread(t, s):
        def step(kk, _):
            LX[t, s - t, kk] = dot(lims[s], sel[t, kk]).astype(BF16)
            return 0

        chunk_loop(step, 0)

    def order(table, b):
        straight = jnp.full((TOK, CH), slot_ref[0, 0]) == 0

        def step(kk, _):
            one = table[b, kk, 0:TOK, :].astype(F32)
            two = table[b, kk, TOK:ROWS, :].astype(F32)
            table[b, kk, 0:TOK, :] = jnp.where(straight, one, two).astype(BF16)
            table[b, kk, TOK:ROWS, :] = jnp.where(straight, two, one).astype(BF16)
            return 0

        chunk_loop(step, 0)

    def recode(value, base, limit):
        base, limit = base.astype(F32), limit.astype(F32)
        delta = jnp.minimum(jnp.maximum(value - base, -limit), limit).astype(BF16)
        return (base + delta.astype(F32)).astype(BF16)

    def cols(kk):
        return pl.ds(pl.multiple_of(kk * CH, CH), CH)

    def flat(s, mat):
        return W[s, mat].reshape(CHUNKS * CH, RANK)

    def forward(s, m):
        hid = activate(s, m)
        wide[...] = dot_t(hid, flat(s, UP))

        def step(kk, sq):
            out = acts[s, kk, rows(m), :].astype(F32) + wide[:, cols(kk)]
            value = recode(out, TB[s, kk, rows(m), :], LX[0, s, kk, rows(m), :])
            acts[s + 1, kk, rows(m), :] = value
            full = value.astype(F32)
            narrow[:, cols(kk)] = (full * gain_row(s + 1, kk)).astype(BF16)
            return sq + fold(full * full)

        sq = chunk_loop(step, zero)
        hand_over(s + 1, m, dot(narrow[...], flat(s + 1, DOWN)), sq)

    def back_first(m):
        def step(kk, carry):
            return carry + dot(ups[3, kk, rows(m), :], rows_of(3, UP, kk))

        xs[4 + 3, m, inner_rows, :] = chunk_loop(step, zero).astype(BF16)
        xb_send(3, m)

    def xb_send(s, m):
        for e in (1, 2, 3):
            remote(
                xs.at[4 + s, m, inner_rows],
                xr.at[4 + s, m, e - 1, inner_rows],
                left.at[L_XB],
                x_r.at[4 + s, m],
                group(e),
            ).start()

    def back_inner(s, m):
        arrived(xr.at[4 + s, m, :, inner_rows], x_r.at[4 + s, m])
        inner, inv = inner_all[s, rows(m), :], inv_all[s, rows(m), :]
        sig = jax.nn.sigmoid(inner)
        bi = x_total(4 + s, m, inner_rows) * sig * (1.0 + inner * (1.0 - sig)) * inv
        bis = bi.astype(BF16)
        bis_all[s, rows(m), :] = bis
        coef = jnp.sum(bis.astype(F32) * inner * inv, axis=-1, keepdims=True) * (1.0 / WIDTH)
        return bis, jnp.broadcast_to(coef, (TOK, CH))

    def backward(s, m):
        bis, coef = back_inner(s, m)
        wide[...] = dot_t(bis, flat(s, DOWN))

        def step(kk, _):
            value = (
                ups[s, kk, rows(m), :].astype(F32)
                + wide[:, cols(kk)] * gain_row(s, kk)
                - acts[s, kk, rows(m), :].astype(F32) * coef
            )
            value = recode(value, GB[s - 1, kk, rows(m), :], LX[1, s - 1, kk, rows(m), :])
            ups[s - 1, kk, rows(m), :] = value
            narrow[:, cols(kk)] = value
            return 0

        chunk_loop(step, 0)
        xs[4 + s - 1, m, inner_rows, :] = dot(narrow[...], flat(s - 1, UP)).astype(BF16)
        xb_send(s - 1, m)

    def keep(s, mat, kk, value):
        value = value.astype(BF16)
        G[s, mat, kk // 2, (kk % 2) * 2] = value[:, :BL]
        G[s, mat, kk // 2, (kk % 2) * 2 + 1] = value[:, BL:]

    def make_grad_up(s):
        turned = jnp.transpose(hid_all[s].astype(F32)).astype(BF16)

        def step(kk, _):
            keep(s, UP, kk, dot(turned, ups[s, kk]))
            return 0

        chunk_loop(step, 0)

    def make_grad_down(s):
        turned = jnp.transpose(bis_all[s].astype(F32)).astype(BF16)

        def step(kk, _):
            keep(s, DOWN, kk, dot(turned, acts[s, kk]) * gain_row(s, kk))
            return 0

        chunk_loop(step, 0)

    rlow, rhigh = pl.ds(0, RANK // 2), pl.ds(RANK // 2, RANK // 2)

    def part(s, mat, o, which):
        if mat == UP:
            return G.at[s, UP, (y + o) % 4, which]
        return G.at[s, DOWN, which, (z + o) % 4]

    def ring(mat):
        return at_y if mat == UP else at_z

    def kind(mat):
        return left.at[L_RU] if mat == UP else left.at[L_RD]

    def grad_down_last():
        make_grad_down(0)
        for d, o in enumerate(OFF):
            remote(
                G.at[0, DOWN, :, (z + o) % 4, rlow], R1a.at[d], left.at[L_RA], a1_r.at[0], at_z(o)
            ).start()
            remote(
                G.at[0, DOWN, (y + o) % 4, :, rhigh], R1h.at[d], left.at[L_RA], g1_r.at[0], at_y(o)
            ).start()

    def send_grad(s, mat):
        for d, o in SIDES:
            remote(part(s, mat, 2, pair(d)), Q.at[s, mat, d], kind(mat), q_r.at[s, mat], ring(mat)(o)).start()
        for d, o in SIDES:
            remote(
                part(s, mat, o, pair(1 - d)),
                R1.at[s, mat, d, pair(1 - d)],
                kind(mat),
                r1_r.at[s, mat],
                ring(mat)(o),
            ).start()

    def relay(s, mat):
        arrived(Q.at[s, mat], q_r.at[s, mat])
        for d, o in SIDES:
            for j in range(2):
                ref = part(s, mat, o, 2 * d + j)
                ref[...] = (ref[...].astype(F32) + Q[s, mat, d, j].astype(F32)).astype(BF16)
            remote(
                part(s, mat, o, pair(d)), R1.at[s, mat, d, pair(d)], kind(mat), r1_r.at[s, mat], ring(mat)(o)
            ).start()

    def add_up(a, parts):
        total = a.astype(F32)
        for value in parts:
            total = total + value.astype(F32)
        return total.astype(BF16)

    def r2(s, mat):
        arrived(R1.at[s, mat], r1_r.at[s, mat])
        for j in range(4):
            S1[s, mat, j] = add_up(part(s, mat, 0, j)[...], [R1[s, mat, d, j] for d in range(2)])
        for d, o in enumerate(OFF):
            there, j = (at_z(o), (z + o) % 4) if mat == UP else (at_y(o), (y + o) % 4)
            remote(S1.at[s, mat, j], R2.at[s, mat, d], left.at[L_R2], r2_r.at[s, mat], there).start()

    def r2_last():
        arrived(R1a, a1_r.at[0])
        for j in range(4):
            S1a[j] = add_up(G[0, DOWN, j, z, rlow, :], [R1a[d, j] for d in range(3)])
        for d, o in enumerate(OFF):
            remote(
                S1a.at[(y + o) % 4], R2.at[0, DOWN, d, rlow], left.at[L_R2], r2_r.at[0, DOWN], at_y(o)
            ).start()
        arrived(R1h, g1_r.at[0])
        for j in range(4):
            S1h[j] = add_up(G[0, DOWN, y, j, rhigh, :], [R1h[d, j] for d in range(3)])
        for d, o in enumerate(OFF):
            remote(
                S1h.at[(z + o) % 4], R2.at[0, DOWN, d, rhigh], left.at[L_R2], r2_r.at[0, DOWN], at_z(o)
            ).start()

    def r3(s, mat):
        arrived(R2.at[s, mat], r2_r.at[s, mat])
        if s == 0 and mat == DOWN:
            for some, own in ((rlow, S1a[y]), (rhigh, S1h[z])):
                S2[s, mat, some, :] = add_up(own, [R2[s, mat, d, some, :] for d in range(3)])
        else:
            own = S1[s, mat, z if mat == UP else y]
            S2[s, mat] = add_up(own, [R2[s, mat, d] for d in range(3)])

        @pl.when(jnp.logical_not(owner_self(s)))
        def _():
            remote(S2.at[s, mat], R3.at[xl, c, mat], left.at[L_R3], r3_r.at[mat], owner(s)).start()

        @pl.when(owner_self(s))
        def _():
            pltpu.make_async_copy(S2.at[s, mat], R3.at[xl, c, mat], r3_r.at[mat]).start()

    def base_ready(table, b, sems):
        arrived(table.at[b], sems.at[b])

    def drain():
        p0_left()
        sent(gains.at[0:3], left.at[L_GAIN])
        sent(lims.at[0:3], left.at[L_LIM])
        pl.when(holds_mid)(lambda: sent(acts, left.at[L_BASE]))
        pl.when(lacks_mid)(lambda: sent(TB.at[0:2], left.at[L_BASE]))
        sent(W.at[0:3, 0, 0:2], left.at[L_W1])
        sent(W.at[0:3, 0, 0:2], left.at[L_W0])
        sent(W.at[0:3, 0, 0:3], left.at[L_WD])
        sent(W.at[0:3, 0, 0:3], left.at[L_WU])
        sent(W.at[0:3, 0], left.at[L_RU])
        sent(W.at[0:3, 0, 0:3], left.at[L_RD])
        sent(W.at[0, 0, 0:3], left.at[L_RA])
        sent(W.at[0:3, 0, 0:2], left.at[L_R2])
        sent(xr.at[0:4], left.at[L_X])
        sent(xr.at[4:8, :, :, inner_rows], left.at[L_XB])

    lax.fori_loop(0, CHUNKS, build_sel, 0)

    def p1_second():
        p1_send(2, DOWN)
        p1_send(2, UP)

    def p1_third():
        p1_send(3, DOWN)
        p1_first(3, UP, 1)

    t_bases()
    holds_late = (xh == 1) & (xl == 1)
    pl.when(holds_late)(p1_second)
    pl.when(holds_late)(p1_third)
    p1_first(0, DOWN, 0)
    p1_send(1, DOWN)
    p1_send(0, UP)
    p1_send(1, UP)
    pl.when(jnp.logical_not(holds_late))(p1_second)
    p2_first(0, DOWN, 0)
    p2_up(0)
    p2_down(1)
    pl.when(jnp.logical_not(holds_late))(p1_third)
    g_bases()
    arrived(gains.at[0:3], gain_r.at[0])
    arrived(lims.at[0:3], lim_r.at[0])
    for s in range(3):
        spread(0, s)
    p2_up(1)
    local_done(acts.at[0], loc_sem.at[0])
    first_ready(0, DOWN, 0)
    first(0)
    first(1)
    p2_down(2)
    p2_up(2)
    g_cross(0, 6)
    for s in range(3):
        base_ready(TB, s, t_ready)
        order(TB, s)
        if s == 2:
            spread(1, 3)
            spread(1, 2)
        up_ready(s)
        down_ready(s + 1)
        forward(s, 0)
        forward(s, 1)
        if s == 0:
            p2_down(3)
            p2_first(3, UP, 1)
        if s < 2:
            g_cross(6 * s + 6, min(6 * s + 12, BLOCKS))
    first_ready(3, UP, 1)
    local_done(ups.at[3], loc_sem.at[1])
    back_first(0)
    back_first(1)
    spread(1, 1)
    activate(3, 0)
    activate(3, 1)
    make_grad_up(3)
    send_grad(3, UP)
    base_ready(GB, 2, g_ready)
    order(GB, 2)
    backward(3, 0)
    backward(3, 1)
    make_grad_down(3)
    send_grad(3, DOWN)
    make_grad_up(2)
    send_grad(2, UP)
    base_ready(GB, 1, g_ready)
    order(GB, 1)
    relay(3, UP)
    backward(2, 0)
    backward(2, 1)
    make_grad_down(2)
    make_grad_up(1)
    relay(3, DOWN)
    send_grad(2, DOWN)
    relay(2, UP)
    send_grad(1, UP)
    base_ready(GB, 0, g_ready)
    order(GB, 0)
    backward(1, 0)
    backward(1, 1)
    r2(3, UP)
    make_grad_down(1)
    make_grad_up(0)
    r2(3, DOWN)
    relay(2, DOWN)
    send_grad(1, DOWN)
    send_grad(0, UP)
    relay(1, UP)
    back_inner(0, 0)
    back_inner(0, 1)
    grad_down_last()
    relay(0, UP)
    relay(1, DOWN)
    r2(2, UP)
    r2(2, DOWN)
    r2(1, UP)
    r2_last()
    r2(1, DOWN)
    r2(0, UP)
    r3(3, UP)
    r3(3, DOWN)
    r3(2, UP)
    r3(2, DOWN)
    r3(1, UP)
    r3(0, DOWN)
    r3(1, DOWN)
    r3(0, UP)
    drain()

    scale = 1.0 / math.sqrt(2 * 2048)
    for mat in (UP, DOWN):
        arrived(R3.at[:, :, mat], r3_r.at[mat])
        for h in (0, 1):
            total = (R3[0, h, mat].astype(F32) + R3[1, h, mat].astype(F32)) * scale
            result[mat, pl.ds(h * BL, BL), :] = jnp.transpose(total)
        pltpu.make_async_copy(result.at[mat], out_hbm.at[mat], out_sem.at[mat]).start()

    pl.when(xl == xh)(lambda: sent(W.at[0, 0, 0:2, 0:3], left.at[L_R3]))
    pl.when(xl != xh)(lambda: sent(W.at[0, 0, 0:2], left.at[L_R3]))
    for mat in (UP, DOWN):
        pltpu.make_async_copy(result.at[mat], out_hbm.at[mat], out_sem.at[mat]).wait()


def split(both_ref, down_ref, up_ref):
    down_ref[0] = both_ref[DOWN]
    up_ref[0] = both_ref[UP]


def body(
    inputs,
    cotangent,
    down_weight,
    up_weight,
    section_gains,
    act_bases,
    grad_bases,
    slot_ids,
    act_exps,
    grad_exps,
):
    any_spec = pl.BlockSpec(memory_space=pl.ANY)
    vmem = pl.BlockSpec(memory_space=pltpu.VMEM)
    dma = pltpu.SemaphoreType.DMA
    both = pl.pallas_call(
        kernel,
        out_shape=jax.ShapeDtypeStruct((2, OWN, RANK), F32),
        in_specs=[any_spec] * 9 + [pl.BlockSpec(memory_space=pltpu.SMEM)],
        out_specs=any_spec,
        scratch_shapes=[
            pltpu.VMEM((4, 2, 4, 4, BL, RANK), BF16),
            pltpu.VMEM((4, CHUNKS, ROWS, CH), BF16),
            pltpu.VMEM((4, CHUNKS, ROWS, CH), BF16),
            pltpu.VMEM((3, CHUNKS, ROWS, CH), BF16),
            pltpu.VMEM((3, CHUNKS, ROWS, CH), BF16),
            pltpu.VMEM((1, WIDTH), BF16),
            pltpu.VMEM((4, CHUNKS, CH), F32),
            pltpu.VMEM((2, ROWS, 64), jnp.int32),
            pltpu.VMEM((4, CHUNKS, CH), F32),
            pltpu.VMEM((4, ROWS, 128), BF16),
            pltpu.VMEM((2, CHUNKS, 128, CH), BF16),
            pltpu.VMEM((8, 2, TOK + 16, 128), BF16),
            pltpu.VMEM((8, 2, 3, TOK + 16, 128), BF16),
            pltpu.VMEM((4, ROWS, RANK), F32),
            pltpu.VMEM((4, ROWS, RANK), F32),
            pltpu.VMEM((4, ROWS, RANK), BF16),
            pltpu.VMEM((4, ROWS, RANK), BF16),
            pltpu.VMEM((4, 2, 4, 4, RANK, BL), BF16),
            pltpu.VMEM((4, 2, 2, 2, RANK, BL), BF16),
            pltpu.VMEM((4, 2, 2, 4, RANK, BL), BF16),
            pltpu.VMEM((4, 2, 4, RANK, BL), BF16),
            pltpu.VMEM((3, 4, RANK // 2, BL), BF16),
            pltpu.VMEM((4, RANK // 2, BL), BF16),
            pltpu.VMEM((3, 4, RANK // 2, BL), BF16),
            pltpu.VMEM((4, RANK // 2, BL), BF16),
            pltpu.VMEM((4, 2, 3, RANK, BL), BF16),
            pltpu.VMEM((4, 2, RANK, BL), BF16),
            pltpu.VMEM((2, 2, 2, RANK, BL), BF16),
            pltpu.VMEM((2, 3, CHUNKS, ROWS, CH), BF16),
            pltpu.VMEM((TOK, CHUNKS * CH), F32),
            pltpu.VMEM((TOK, CHUNKS * CH), BF16),
            pltpu.VMEM((2, OWN, RANK), F32),
            dma((2,)),
            dma((4,)),
            dma((3,)),
            dma((3,)),
            dma((1,)),
            dma((1,)),
            dma((4, 2)),
            dma((4, 2)),
            dma((2,)),
            dma((2,)),
            dma((4, 2)),
            dma((4, 2)),
            dma((4, 2)),
            dma((1,)),
            dma((1,)),
            dma((4, 2)),
            dma((2,)),
            dma((8, 2)),
            dma((LEFT_KINDS,)),
        ],
        compiler_params=pltpu.CompilerParams(
            collective_id=0, has_side_effects=True, vmem_limit_bytes=56 * 2**20
        ),
    )(
        inputs.reshape(ROWS, WIDTH),
        cotangent.reshape(ROWS, WIDTH),
        down_weight[0],
        up_weight[0],
        act_bases.reshape(2, ROWS, WIDTH),
        grad_bases.reshape(2, ROWS, WIDTH),
        section_gains,
        act_exps.reshape(ROWS, 64),
        grad_exps.reshape(ROWS, 64),
        slot_ids,
    )
    grad_down, grad_up = pl.pallas_call(
        split,
        out_shape=(jax.ShapeDtypeStruct((1, OWN, RANK), F32),) * 2,
        in_specs=[vmem],
        out_specs=(vmem, vmem),
    )(both)
    return grad_down, grad_up


def solution(mesh):
    return jax.shard_map(
        body,
        mesh=mesh,
        in_specs=(
            P(None, "dp", None),
            P(None, "dp", None),
            P("section", "dp", None),
            P("section", "dp", None),
            P("section", None),
            P("section", None, None, "dp", None),
            P("section", None, None, "dp", None),
            P("dp", None),
            P("section", None, "dp", None),
            P("section", None, "dp", None),
        ),
        out_specs=(P("section", "dp", None), P("section", "dp", None)),
        check_vma=False,
    )
```

```python
import functools
import math

import jax
import jax.numpy as jnp
from jax import lax
from jax.experimental import pallas as pl
from jax.experimental.pallas import tpu as pltpu
from jax.sharding import PartitionSpec as P

MESH = pl.DeviceIdType.MESH
F32 = jnp.float32
BF16 = jnp.bfloat16

SECTIONS = 4
WIDTH = 8192
RANK = 128
TOK = 64
ROWS = 2 * TOK
OWN = 256
BL = 128
BLOCKS = 16
CH = 2 * BL
CHUNKS = 8
NORM_EPS = 1e-05
OFF = (1, 3, 2)
DOWN, UP = 0, 1
(
    L_P0,
    L_GAIN,
    L_LIM,
    L_BASE,
    L_W1,
    L_W0,
    L_WD,
    L_WU,
    L_RU,
    L_RD,
    L_RA,
    L_R2,
    L_R3,
    L_X,
    L_XB,
    LEFT_KINDS,
) = range(16)


def dot(a, b):
    return jnp.dot(a, b, preferred_element_type=F32)


def dot_t(a, b):
    return lax.dot_general(a, b, (((1,), (1,)), ((), ())), preferred_element_type=F32)


def kernel(
    x_hbm,
    ct_hbm,
    dw_hbm,
    uw_hbm,
    ab_hbm,
    gb_hbm,
    gain_hbm,
    ae_hbm,
    ge_hbm,
    slot_ref,
    out_hbm,
    W,
    acts,
    ups,
    TB,
    GB,
    gain_in,
    gain_out,
    exps_in,
    gains,
    lims,
    sel,
    xs,
    xr,
    inner_all,
    inv_all,
    hid_all,
    bis_all,
    G,
    Q,
    R1,
    S1,
    R1a,
    S1a,
    R1h,
    S1h,
    R2,
    S2,
    R3,
    LX,
    wide,
    narrow,
    result,
    held,
    held_sem,
    out_sem,
    loc_sem,
    t_ready,
    g_ready,
    gain_r,
    lim_r,
    p0_r,
    p1_r,
    h1_r,
    h2_r,
    p2_r,
    q_r,
    r1_r,
    a1_r,
    g1_r,
    r2_r,
    r3_r,
    x_r,
    left,
):
    S, J = lax.axis_index("section"), lax.axis_index("dp")
    xh, c = S // 2, S % 2
    y, xl, z = J // 8, (J // 4) % 2, J % 4

    def dp(yy, xx, zz):
        return yy * 8 + xx * 4 + zz

    def at_y(o):
        return (S, dp((y + o) % 4, xl, z))

    def at_z(o):
        return (S, dp(y, xl, (z + o) % 4))

    def group(e):
        return ((S + e) % 4, J)

    def p0_dev(xx, h):
        return (xl * 2 + h, dp(y, xx, z))

    def p0_self(xx, h):
        return (xl * 2 + h == S) & (xl == xx)

    def owner(s):
        return (s, dp(y, xh, z))

    def owner_self(s):
        return (S == s) & (xl == xh)

    def feat(k, h, cc):
        return (k // 4) * 2048 + h * 1024 + (k % 4) * OWN + cc * BL

    def remote(a, b, ss, rs, dev):
        return pltpu.make_async_remote_copy(
            src_ref=a, dst_ref=b, send_sem=ss, recv_sem=rs, device_id=dev, device_id_type=MESH
        )

    def arrived(ref, rs):
        remote(ref, ref, rs, rs, (S, J)).wait_recv()

    def sent(ref, ss):
        remote(ref, ref, ss, ss, (S, J)).wait_send()

    def local_done(ref, sem):
        pltpu.make_async_copy(ref, ref, sem).wait()

    barrier = pltpu.get_barrier_semaphore()

    def greet(dev):
        pl.semaphore_signal(barrier, inc=1, device_id=dev, device_id_type=MESH)

    def greet_all():
        for e in (1, 2, 3):
            greet(group(e))
            greet(at_y(e))
            greet(at_z(e))
        for xx in (0, 1):
            for h in (0, 1):
                @pl.when(jnp.logical_not(p0_self(xx, h)))
                def _():
                    greet(p0_dev(xx, h))
        for s in range(SECTIONS):
            @pl.when(jnp.logical_not(owner_self(s)))
            def _():
                greet(owner(s))

    def place(ref_of, dst, k, h, cc):
        return (
            ref_of.at[:, pl.ds(pl.multiple_of(feat(k, h, cc), BL), BL)],
            dst.at[k // 2, :, pl.ds(pl.multiple_of((k % 2) * BL, BL), BL)],
        )

    def load(ref_of, dst, sem, h, cc):
        def step(k, _):
            pltpu.make_async_copy(*place(ref_of, dst, k, h, cc), sem).start()
            return 0

        lax.fori_loop(0, BLOCKS, step, 0)

    def push(ref_of, dst, ss, rs, h, cc, dev, lo, hi):
        def step(k, _):
            remote(*place(ref_of, dst, k, h, cc), ss, rs, dev).start()
            return 0

        lax.fori_loop(lo, hi, step, 0)

    near = 2 * xh
    holds_mid = c != xh
    lacks_mid = c == xh
    cross = (S + 2) % 4
    sib = xh * 2 + (1 - c)

    for mat, ref in ((DOWN, dw_hbm), (UP, uw_hbm)):
        pltpu.make_async_copy(ref, held.at[mat], held_sem.at[mat]).start()
    greet_all()
    pltpu.make_async_copy(gain_hbm, gain_in, loc_sem.at[2]).start()
    pltpu.make_async_copy(ae_hbm, exps_in.at[0], loc_sem.at[3]).start()
    pltpu.make_async_copy(ge_hbm, exps_in.at[1], loc_sem.at[3]).start()
    load(x_hbm, acts.at[0], loc_sem.at[0], xh, c)
    pl.semaphore_wait(barrier, 9 + 8 - 2 * jnp.where(xl == xh, 1, 0))

    def p0_send(mat):
        for xx in (0, 1):
            for h in (0, 1):
                here, there = held.at[mat, pl.ds(h * BL, BL)], W.at[S, mat, y, z]

                @pl.when(jnp.logical_not(p0_self(xx, h)))
                def _():
                    remote(here, there, left.at[L_P0], p0_r.at[S, mat], p0_dev(xx, h)).start()

                @pl.when(p0_self(xx, h))
                def _():
                    pltpu.make_async_copy(here, there, p0_r.at[S, mat]).start()

    local_done(held.at[DOWN], held_sem.at[DOWN])
    pl.when(c == 0)(lambda: p0_send(DOWN))

    pltpu.make_async_copy(gain_hbm, gain_in, loc_sem.at[2]).wait()
    for dst in range(SECTIONS):
        for kk in range(CHUNKS):
            for j in (0, 1):
                row = gain_in[:, pl.ds(feat(2 * kk + j, dst // 2, dst % 2), BL)].astype(F32)
                gain_out[dst, pl.ds(kk, 1), pl.ds(j * BL, BL)] = row
    gains[S] = gain_out[S]
    local_done(exps_in, loc_sem.at[3])
    exps = jnp.concatenate([exps_in[0], exps_in[1]], axis=1)
    limit = jnp.full((ROWS, 128), 448.0 * 2.0**-6, F32)
    for e in (7, 8, 9):
        limit = jnp.where(exps == e, 448.0 * 2.0**-e, limit)
    lims[S] = limit.astype(BF16)
    pl.when(c == 1)(lambda: p0_send(DOWN))
    local_done(held.at[UP], held_sem.at[UP])
    p0_send(UP)
    for e in (1, 2, 3):
        remote(gain_out.at[(S + e) % 4], gains.at[S], left.at[L_GAIN], gain_r.at[0], group(e)).start()
        remote(lims.at[S], lims.at[S], left.at[L_LIM], lim_r.at[0], group(e)).start()

    def build_sel(kk, _):
        b0 = (kk // 2) * 16 + xh * 8 + (kk % 2) * 4 + c
        row = lax.broadcasted_iota(jnp.int32, (128, CH), 0)
        blk = (lax.broadcasted_iota(jnp.int32, (128, CH), 1) // BL) * 2 + b0
        sel[0, kk] = jnp.where(row == blk, 1.0, 0.0).astype(BF16)
        sel[1, kk] = jnp.where(row == blk + 64, 1.0, 0.0).astype(BF16)
        return 0

    def t_bases():
        push(ab_hbm.at[1 - c], TB.at[near], left.at[L_BASE], t_ready.at[near], 1 - xh, c, (cross, J), 0, BLOCKS)
        load(ab_hbm.at[1 - c], TB.at[near], t_ready.at[near], xh, c)

        @pl.when(holds_mid)
        def _():
            push(ab_hbm.at[c], TB.at[1], left.at[L_BASE], t_ready.at[1], xh, 1 - c, (sib, J), 0, BLOCKS)
            load(ab_hbm.at[c], TB.at[1], t_ready.at[1], xh, c)

    def g_bases():
        load(ct_hbm, ups.at[3], loc_sem.at[1], xh, c)
        load(gb_hbm.at[1 - c], GB.at[near], g_ready.at[near], xh, c)

        @pl.when(holds_mid)
        def _():
            push(gb_hbm.at[c], GB.at[1], left.at[L_BASE], g_ready.at[1], xh, 1 - c, (sib, J), 0, BLOCKS)
            load(gb_hbm.at[c], GB.at[1], g_ready.at[1], xh, c)

    def g_cross(lo, hi):
        push(gb_hbm.at[1 - c], GB.at[near], left.at[L_BASE], g_ready.at[near], 1 - xh, c, (cross, J), lo, hi)

    def p0_left():
        pl.when(xl == xh)(lambda: sent(W.at[0, 0, 0:2, 0:3], left.at[L_P0]))
        pl.when(xl != xh)(lambda: sent(W.at[0, 0, 0:2], left.at[L_P0]))

    half = BL // 2
    low, high = pl.ds(0, half), pl.ds(half, half)
    SIDES = ((0, 1), (1, 3))

    def p1_send(s, mat):
        w = W.at[s, mat, y, z]
        arrived(w, p0_r.at[s, mat])
        for o in OFF:
            there = at_y(o) if mat == DOWN else at_z(o)
            remote(w, w, left.at[L_W1], p1_r.at[s, mat], there).start()

    def p1_first(s, mat, i):
        w = W.at[s, mat, y, z]
        arrived(w, p0_r.at[s, mat])
        for o in OFF:
            v = w.at[low]
            remote(v, v, left.at[L_W1], p1_r.at[s, mat], at_y(o)).start()
            v = w.at[high]
            remote(v, v, left.at[L_W1], h1_r.at[i], at_z(o)).start()

    def p2_first(s, mat, i):
        arrived(W.at[s, mat, 0:3, 0, low], p1_r.at[s, mat])
        for o in OFF:
            w = W.at[s, mat, :, z, low]
            remote(w, w, left.at[L_W0], p2_r.at[s, mat], at_z(o)).start()
        arrived(W.at[s, mat, 0, 0:3, high], h1_r.at[i])
        for o in OFF:
            w = W.at[s, mat, y, :, high]
            remote(w, w, left.at[L_W0], h2_r.at[i], at_y(o)).start()

    def first_ready(s, mat, i):
        arrived(W.at[s, mat, :, 0:3, low], p2_r.at[s, mat])
        arrived(W.at[s, mat, 0:3, :, high], h2_r.at[i])

    def p2_down(s):
        arrived(W.at[s, DOWN, 0:3, 0], p1_r.at[s, DOWN])
        for o in OFF:
            w = W.at[s, DOWN, :, z]
            remote(w, w, left.at[L_WD], p2_r.at[s, DOWN], at_z(o)).start()

    def down_ready(s):
        arrived(W.at[s, DOWN, :, 0:3], p2_r.at[s, DOWN])

    def p2_up(s):
        arrived(W.at[s, UP, 0, 0:3], p1_r.at[s, UP])
        for o in OFF:
            w = W.at[s, UP, y]
            remote(w, w, left.at[L_WU], p2_r.at[s, UP], at_y(o)).start()

    def up_ready(s):
        arrived(W.at[s, UP, 0:3], p2_r.at[s, UP])

    def pair(d):
        return pl.ds(2 * d, 2)

    def rows(m):
        return pl.ds(m * TOK, TOK)

    def gain_row(s, kk):
        return gains[s, pl.ds(kk, 1), :]

    def rows_of(s, mat, kk):
        return W[s, mat, kk // 2, pl.ds((kk % 2) * 2, 2)].reshape(CH, RANK)

    def fold(v):
        return v[:, :128] + v[:, 128:]

    def chunk_loop(step, init):
        return lax.fori_loop(0, CHUNKS, step, init, unroll=True)

    def x_send(ex, m):
        for e in (2, 3, 1):
            remote(
                xs.at[ex, m], xr.at[ex, m, e - 1], left.at[L_X], x_r.at[ex, m], group(e)
            ).start()

    inner_rows, square_rows = pl.ds(0, TOK), pl.ds(TOK, 16)

    def x_total(ex, m, part):
        total = xs[ex, m, part, :].astype(F32)
        for e in range(3):
            total = total + xr[ex, m, e, part, :].astype(F32)
        return total

    def diagonal(v):
        shape = (TOK, 128)
        here = lax.broadcasted_iota(jnp.int32, shape, 0) == lax.broadcasted_iota(jnp.int32, shape, 1)
        return jnp.where(here, v, 0.0)

    def x_wait(ex, m):
        arrived(xr.at[ex, m], x_r.at[ex, m])

    zero = jnp.zeros((TOK, 128), F32)

    def enter(s, kk, value, inner, sq):
        full = value.astype(F32)
        sq = sq + fold(full * full)
        scaled = (full * gain_row(s, kk)).astype(BF16)
        return inner + dot(scaled, rows_of(s, DOWN, kk)), sq

    def hand_over(ex, m, inner, sq):
        row = jnp.sum(diagonal(jnp.sum(sq, axis=-1, keepdims=True)), axis=0, keepdims=True)
        coarse = row.astype(BF16).astype(F32)
        upper = lax.broadcasted_iota(jnp.int32, (16, 128), 0) < 8
        xs[ex, m, inner_rows, :] = inner.astype(BF16)
        xs[ex, m, square_rows, :] = jnp.where(upper, coarse, row - coarse).astype(BF16)
        x_send(ex, m)

    def first(m):
        def step(kk, carry):
            return enter(0, kk, acts[0, kk, rows(m), :], *carry)

        inner, sq = chunk_loop(step, (zero, zero))
        hand_over(0, m, inner, sq)

    def activate(s, m):
        x_wait(s, m)
        squares = x_total(s, m, square_rows)
        row = squares[0:1, :] + squares[8:9, :]
        mean = jnp.sum(diagonal(row), axis=-1, keepdims=True) * (1.0 / WIDTH)
        inv = jnp.broadcast_to(lax.rsqrt(mean + NORM_EPS), (TOK, 128))
        inner = x_total(s, m, inner_rows) * inv
        hid = (inner * jax.nn.sigmoid(inner)).astype(BF16)
        inner_all[s, rows(m), :] = inner
        inv_all[s, rows(m), :] = inv
        hid_all[s, rows(m), :] = hid
        return hid

    def spread(t, s):
        def step(kk, _):
            LX[t, s - t, kk] = dot(lims[s], sel[t, kk]).astype(BF16)
            return 0

        chunk_loop(step, 0)

    def order(table, b):
        straight = jnp.full((TOK, CH), slot_ref[0, 0]) == 0

        def step(kk, _):
            one = table[b, kk, 0:TOK, :].astype(F32)
            two = table[b, kk, TOK:ROWS, :].astype(F32)
            table[b, kk, 0:TOK, :] = jnp.where(straight, one, two).astype(BF16)
            table[b, kk, TOK:ROWS, :] = jnp.where(straight, two, one).astype(BF16)
            return 0

        chunk_loop(step, 0)

    def recode(value, base, limit):
        base, limit = base.astype(F32), limit.astype(F32)
        delta = jnp.minimum(jnp.maximum(value - base, -limit), limit).astype(BF16)
        return (base + delta.astype(F32)).astype(BF16)

    def cols(kk):
        return pl.ds(pl.multiple_of(kk * CH, CH), CH)

    def flat(s, mat):
        return W[s, mat].reshape(CHUNKS * CH, RANK)

    def forward(s, m):
        hid = activate(s, m)
        wide[...] = dot_t(hid, flat(s, UP))

        def step(kk, sq):
            out = acts[s, kk, rows(m), :].astype(F32) + wide[:, cols(kk)]
            value = recode(out, TB[s, kk, rows(m), :], LX[0, s, kk, rows(m), :])
            acts[s + 1, kk, rows(m), :] = value
            full = value.astype(F32)
            narrow[:, cols(kk)] = (full * gain_row(s + 1, kk)).astype(BF16)
            return sq + fold(full * full)

        sq = chunk_loop(step, zero)
        hand_over(s + 1, m, dot(narrow[...], flat(s + 1, DOWN)), sq)

    def back_first(m):
        def step(kk, carry):
            return carry + dot(ups[3, kk, rows(m), :], rows_of(3, UP, kk))

        xs[4 + 3, m, inner_rows, :] = chunk_loop(step, zero).astype(BF16)
        xb_send(3, m)

    def xb_send(s, m):
        for e in (2, 3, 1):
            remote(
                xs.at[4 + s, m, inner_rows],
                xr.at[4 + s, m, e - 1, inner_rows],
                left.at[L_XB],
                x_r.at[4 + s, m],
                group(e),
            ).start()

    def back_inner(s, m):
        arrived(xr.at[4 + s, m, :, inner_rows], x_r.at[4 + s, m])
        inner, inv = inner_all[s, rows(m), :], inv_all[s, rows(m), :]
        sig = jax.nn.sigmoid(inner)
        bi = x_total(4 + s, m, inner_rows) * sig * (1.0 + inner * (1.0 - sig)) * inv
        bis = bi.astype(BF16)
        bis_all[s, rows(m), :] = bis
        coef = jnp.sum(bis.astype(F32) * inner * inv, axis=-1, keepdims=True) * (1.0 / WIDTH)
        return bis, jnp.broadcast_to(coef, (TOK, CH))

    def backward(s, m):
        bis, coef = back_inner(s, m)
        wide[...] = dot_t(bis, flat(s, DOWN))

        def step(kk, _):
            value = (
                ups[s, kk, rows(m), :].astype(F32)
                + wide[:, cols(kk)] * gain_row(s, kk)
                - acts[s, kk, rows(m), :].astype(F32) * coef
            )
            value = recode(value, GB[s - 1, kk, rows(m), :], LX[1, s - 1, kk, rows(m), :])
            ups[s - 1, kk, rows(m), :] = value
            narrow[:, cols(kk)] = value
            return 0

        chunk_loop(step, 0)
        xs[4 + s - 1, m, inner_rows, :] = dot(narrow[...], flat(s - 1, UP)).astype(BF16)
        xb_send(s - 1, m)

    def keep(s, mat, kk, value):
        value = value.astype(BF16)
        G[s, mat, kk // 2, (kk % 2) * 2] = value[:, :BL]
        G[s, mat, kk // 2, (kk % 2) * 2 + 1] = value[:, BL:]

    def make_grad_up(s):
        turned = jnp.transpose(hid_all[s].astype(F32)).astype(BF16)

        def step(kk, _):
            keep(s, UP, kk, dot(turned, ups[s, kk]))
            return 0

        chunk_loop(step, 0)

    def make_grad_down(s):
        turned = jnp.transpose(bis_all[s].astype(F32)).astype(BF16)

        def step(kk, _):
            keep(s, DOWN, kk, dot(turned, acts[s, kk]) * gain_row(s, kk))
            return 0

        chunk_loop(step, 0)

    rlow, rhigh = pl.ds(0, RANK // 2), pl.ds(RANK // 2, RANK // 2)

    def part(s, mat, o, which):
        if mat == UP:
            return G.at[s, UP, (y + o) % 4, which]
        return G.at[s, DOWN, which, (z + o) % 4]

    def ring(mat):
        return at_y if mat == UP else at_z

    def kind(mat):
        return left.at[L_RU] if mat == UP else left.at[L_RD]

    def grad_down_last():
        make_grad_down(0)
        for d, o in enumerate(OFF):
            remote(
                G.at[0, DOWN, :, (z + o) % 4, rlow], R1a.at[d], left.at[L_RA], a1_r.at[0], at_z(o)
            ).start()
            remote(
                G.at[0, DOWN, (y + o) % 4, :, rhigh], R1h.at[d], left.at[L_RA], g1_r.at[0], at_y(o)
            ).start()

    def send_grad(s, mat):
        for d, o in SIDES:
            remote(part(s, mat, 2, pair(d)), Q.at[s, mat, d], kind(mat), q_r.at[s, mat], ring(mat)(o)).start()
        for d, o in SIDES:
            remote(
                part(s, mat, o, pair(1 - d)),
                R1.at[s, mat, d, pair(1 - d)],
                kind(mat),
                r1_r.at[s, mat],
                ring(mat)(o),
            ).start()

    def relay(s, mat):
        arrived(Q.at[s, mat], q_r.at[s, mat])
        for d, o in SIDES:
            for j in range(2):
                ref = part(s, mat, o, 2 * d + j)
                ref[...] = (ref[...].astype(F32) + Q[s, mat, d, j].astype(F32)).astype(BF16)
            remote(
                part(s, mat, o, pair(d)), R1.at[s, mat, d, pair(d)], kind(mat), r1_r.at[s, mat], ring(mat)(o)
            ).start()

    def add_up(a, parts):
        total = a.astype(F32)
        for value in parts:
            total = total + value.astype(F32)
        return total.astype(BF16)

    def r2(s, mat):
        arrived(R1.at[s, mat], r1_r.at[s, mat])
        for j in range(4):
            S1[s, mat, j] = add_up(part(s, mat, 0, j)[...], [R1[s, mat, d, j] for d in range(2)])
        for d, o in enumerate(OFF):
            there, j = (at_z(o), (z + o) % 4) if mat == UP else (at_y(o), (y + o) % 4)
            remote(S1.at[s, mat, j], R2.at[s, mat, d], left.at[L_R2], r2_r.at[s, mat], there).start()

    def r2_last():
        arrived(R1a, a1_r.at[0])
        for j in range(4):
            S1a[j] = add_up(G[0, DOWN, j, z, rlow, :], [R1a[d, j] for d in range(3)])
        for d, o in enumerate(OFF):
            remote(
                S1a.at[(y + o) % 4], R2.at[0, DOWN, d, rlow], left.at[L_R2], r2_r.at[0, DOWN], at_y(o)
            ).start()
        arrived(R1h, g1_r.at[0])
        for j in range(4):
            S1h[j] = add_up(G[0, DOWN, y, j, rhigh, :], [R1h[d, j] for d in range(3)])
        for d, o in enumerate(OFF):
            remote(
                S1h.at[(z + o) % 4], R2.at[0, DOWN, d, rhigh], left.at[L_R2], r2_r.at[0, DOWN], at_z(o)
            ).start()

    def r3(s, mat):
        arrived(R2.at[s, mat], r2_r.at[s, mat])
        if s == 0 and mat == DOWN:
            for some, own in ((rlow, S1a[y]), (rhigh, S1h[z])):
                S2[s, mat, some, :] = add_up(own, [R2[s, mat, d, some, :] for d in range(3)])
        else:
            own = S1[s, mat, z if mat == UP else y]
            S2[s, mat] = add_up(own, [R2[s, mat, d] for d in range(3)])

        @pl.when(jnp.logical_not(owner_self(s)))
        def _():
            remote(S2.at[s, mat], R3.at[xl, c, mat], left.at[L_R3], r3_r.at[mat], owner(s)).start()

        @pl.when(owner_self(s))
        def _():
            pltpu.make_async_copy(S2.at[s, mat], R3.at[xl, c, mat], r3_r.at[mat]).start()

    def base_ready(table, b, sems):
        arrived(table.at[b], sems.at[b])

    def drain():
        p0_left()
        sent(gains.at[0:3], left.at[L_GAIN])
        sent(lims.at[0:3], left.at[L_LIM])
        pl.when(holds_mid)(lambda: sent(acts, left.at[L_BASE]))
        pl.when(lacks_mid)(lambda: sent(TB.at[0:2], left.at[L_BASE]))
        sent(W.at[0:3, 0, 0:2], left.at[L_W1])
        sent(W.at[0:3, 0, 0:2], left.at[L_W0])
        sent(W.at[0:3, 0, 0:3], left.at[L_WD])
        sent(W.at[0:3, 0, 0:3], left.at[L_WU])
        sent(W.at[0:3, 0], left.at[L_RU])
        sent(W.at[0:3, 0, 0:3], left.at[L_RD])
        sent(W.at[0, 0, 0:3], left.at[L_RA])
        sent(W.at[0:3, 0, 0:2], left.at[L_R2])
        sent(xr.at[0:4], left.at[L_X])
        sent(xr.at[4:8, :, :, inner_rows], left.at[L_XB])

    lax.fori_loop(0, CHUNKS, build_sel, 0)

    def p1_second():
        p1_send(2, DOWN)
        p1_send(2, UP)

    def p1_third():
        p1_send(3, DOWN)
        p1_first(3, UP, 1)

    t_bases()
    holds_late = (xh == 1) & (xl == 1)
    pl.when(holds_late)(p1_second)
    pl.when(holds_late)(p1_third)
    p1_first(0, DOWN, 0)
    p1_send(1, DOWN)
    p1_send(0, UP)
    p1_send(1, UP)
    pl.when(jnp.logical_not(holds_late))(p1_second)
    p2_first(0, DOWN, 0)
    p2_up(0)
    p2_down(1)
    pl.when(jnp.logical_not(holds_late))(p1_third)
    g_bases()
    arrived(gains.at[0:3], gain_r.at[0])
    arrived(lims.at[0:3], lim_r.at[0])
    for s in range(3):
        spread(0, s)
    p2_up(1)
    local_done(acts.at[0], loc_sem.at[0])
    first_ready(0, DOWN, 0)
    first(0)
    first(1)
    p2_down(2)
    p2_up(2)
    g_cross(0, 6)
    for s in range(3):
        base_ready(TB, s, t_ready)
        order(TB, s)
        if s == 2:
            spread(1, 3)
            spread(1, 2)
        up_ready(s)
        down_ready(s + 1)
        forward(s, 0)
        forward(s, 1)
        if s == 0:
            p2_down(3)
            p2_first(3, UP, 1)
        if s < 2:
            g_cross(6 * s + 6, min(6 * s + 12, BLOCKS))
    first_ready(3, UP, 1)
    local_done(ups.at[3], loc_sem.at[1])
    back_first(0)
    back_first(1)
    spread(1, 1)
    activate(3, 0)
    activate(3, 1)
    make_grad_up(3)
    send_grad(3, UP)
    base_ready(GB, 2, g_ready)
    order(GB, 2)
    backward(3, 0)
    backward(3, 1)
    make_grad_down(3)
    send_grad(3, DOWN)
    make_grad_up(2)
    send_grad(2, UP)
    base_ready(GB, 1, g_ready)
    order(GB, 1)
    relay(3, UP)
    backward(2, 0)
    backward(2, 1)
    make_grad_down(2)
    make_grad_up(1)
    relay(3, DOWN)
    send_grad(2, DOWN)
    relay(2, UP)
    send_grad(1, UP)
    base_ready(GB, 0, g_ready)
    order(GB, 0)
    backward(1, 0)
    backward(1, 1)
    r2(3, UP)
    make_grad_down(1)
    make_grad_up(0)
    r2(3, DOWN)
    send_grad(1, DOWN)
    send_grad(0, UP)
    back_inner(0, 0)
    back_inner(0, 1)
    grad_down_last()
    relay(2, DOWN)
    relay(1, UP)
    r3(3, UP)
    r3(3, DOWN)
    relay(0, UP)
    relay(1, DOWN)
    r2(2, UP)
    r2_last()
    r2(2, DOWN)
    r2(1, UP)
    r2(1, DOWN)
    r2(0, UP)
    r3(2, UP)
    r3(2, DOWN)
    r3(1, UP)
    r3(0, DOWN)
    r3(1, DOWN)
    r3(0, UP)
    drain()

    scale = 1.0 / math.sqrt(2 * 2048)
    for mat in (UP, DOWN):
        arrived(R3.at[:, :, mat], r3_r.at[mat])
        for h in (0, 1):
            total = (R3[0, h, mat].astype(F32) + R3[1, h, mat].astype(F32)) * scale
            result[mat, pl.ds(h * BL, BL), :] = jnp.transpose(total)
        pltpu.make_async_copy(result.at[mat], out_hbm.at[mat], out_sem.at[mat]).start()

    pl.when(xl == xh)(lambda: sent(W.at[0, 0, 0:2, 0:3], left.at[L_R3]))
    pl.when(xl != xh)(lambda: sent(W.at[0, 0, 0:2], left.at[L_R3]))
    for mat in (UP, DOWN):
        pltpu.make_async_copy(result.at[mat], out_hbm.at[mat], out_sem.at[mat]).wait()


def split(both_ref, down_ref, up_ref):
    down_ref[0] = both_ref[DOWN]
    up_ref[0] = both_ref[UP]


def body(
    inputs,
    cotangent,
    down_weight,
    up_weight,
    section_gains,
    act_bases,
    grad_bases,
    slot_ids,
    act_exps,
    grad_exps,
):
    any_spec = pl.BlockSpec(memory_space=pl.ANY)
    vmem = pl.BlockSpec(memory_space=pltpu.VMEM)
    dma = pltpu.SemaphoreType.DMA
    both = pl.pallas_call(
        kernel,
        out_shape=jax.ShapeDtypeStruct((2, OWN, RANK), F32),
        in_specs=[any_spec] * 9 + [pl.BlockSpec(memory_space=pltpu.SMEM)],
        out_specs=any_spec,
        scratch_shapes=[
            pltpu.VMEM((4, 2, 4, 4, BL, RANK), BF16),
            pltpu.VMEM((4, CHUNKS, ROWS, CH), BF16),
            pltpu.VMEM((4, CHUNKS, ROWS, CH), BF16),
            pltpu.VMEM((3, CHUNKS, ROWS, CH), BF16),
            pltpu.VMEM((3, CHUNKS, ROWS, CH), BF16),
            pltpu.VMEM((1, WIDTH), BF16),
            pltpu.VMEM((4, CHUNKS, CH), F32),
            pltpu.VMEM((2, ROWS, 64), jnp.int32),
            pltpu.VMEM((4, CHUNKS, CH), F32),
            pltpu.VMEM((4, ROWS, 128), BF16),
            pltpu.VMEM((2, CHUNKS, 128, CH), BF16),
            pltpu.VMEM((8, 2, TOK + 16, 128), BF16),
            pltpu.VMEM((8, 2, 3, TOK + 16, 128), BF16),
            pltpu.VMEM((4, ROWS, RANK), F32),
            pltpu.VMEM((4, ROWS, RANK), F32),
            pltpu.VMEM((4, ROWS, RANK), BF16),
            pltpu.VMEM((4, ROWS, RANK), BF16),
            pltpu.VMEM((4, 2, 4, 4, RANK, BL), BF16),
            pltpu.VMEM((4, 2, 2, 2, RANK, BL), BF16),
            pltpu.VMEM((4, 2, 2, 4, RANK, BL), BF16),
            pltpu.VMEM((4, 2, 4, RANK, BL), BF16),
            pltpu.VMEM((3, 4, RANK // 2, BL), BF16),
            pltpu.VMEM((4, RANK // 2, BL), BF16),
            pltpu.VMEM((3, 4, RANK // 2, BL), BF16),
            pltpu.VMEM((4, RANK // 2, BL), BF16),
            pltpu.VMEM((4, 2, 3, RANK, BL), BF16),
            pltpu.VMEM((4, 2, RANK, BL), BF16),
            pltpu.VMEM((2, 2, 2, RANK, BL), BF16),
            pltpu.VMEM((2, 3, CHUNKS, ROWS, CH), BF16),
            pltpu.VMEM((TOK, CHUNKS * CH), F32),
            pltpu.VMEM((TOK, CHUNKS * CH), BF16),
            pltpu.VMEM((2, OWN, RANK), F32),
            pltpu.VMEM((2, OWN, RANK), BF16),
            dma((2,)),
            dma((2,)),
            dma((4,)),
            dma((3,)),
            dma((3,)),
            dma((1,)),
            dma((1,)),
            dma((4, 2)),
            dma((4, 2)),
            dma((2,)),
            dma((2,)),
            dma((4, 2)),
            dma((4, 2)),
            dma((4, 2)),
            dma((1,)),
            dma((1,)),
            dma((4, 2)),
            dma((2,)),
            dma((8, 2)),
            dma((LEFT_KINDS,)),
        ],
        compiler_params=pltpu.CompilerParams(
            collective_id=0, has_side_effects=True, vmem_limit_bytes=56 * 2**20
        ),
    )(
        inputs.reshape(ROWS, WIDTH),
        cotangent.reshape(ROWS, WIDTH),
        down_weight[0],
        up_weight[0],
        act_bases.reshape(2, ROWS, WIDTH),
        grad_bases.reshape(2, ROWS, WIDTH),
        section_gains,
        act_exps.reshape(ROWS, 64),
        grad_exps.reshape(ROWS, 64),
        slot_ids,
    )
    grad_down, grad_up = pl.pallas_call(
        split,
        out_shape=(jax.ShapeDtypeStruct((1, OWN, RANK), F32),) * 2,
        in_specs=[vmem],
        out_specs=(vmem, vmem),
    )(both)
    return grad_down, grad_up


def solution(mesh):
    return jax.shard_map(
        body,
        mesh=mesh,
        in_specs=(
            P(None, "dp", None),
            P(None, "dp", None),
            P("section", "dp", None),
            P("section", "dp", None),
            P("section", None),
            P("section", None, None, "dp", None),
            P("section", None, None, "dp", None),
            P("dp", None),
            P("section", None, "dp", None),
            P("section", None, "dp", None),
        ),
        out_specs=(P("section", "dp", None), P("section", "dp", None)),
        check_vma=False,
    )
```
